128 devices in a mesh: depth: 2 (over core), batch: 64 (over z, y, x).
Axes of the slice: x: 4, y: 4, z: 4, core: 2. Of those that a mesh axis runs over, the one named last changes fastest.
Arguments:
- initial: float32 [64, 32, 32, 128], P('batch'), may hold values from -18 to 18
- guess: float32 [2, 64, 32, 32, 128], P('depth', 'batch'), may hold values from -6 to 6
- conv_in: float32 [8, 3, 3, 128, 128], P('depth'), may hold values from -0.1875 to 0.1875
- conv_out: float32 [8, 3, 3, 128, 128], P('depth'), may hold values from -0.1875 to 0.1875
Outputs:
- corrected: float32 [2, 64, 32, 32, 128], P('depth', 'batch')
- relaxed: float32 [2, 64, 32, 32, 128], P('depth', 'batch')
The draws below stay inside these ranges and needn't reach their ends.
All inputs are finite; a program needn't handle non-finite values.
Results may differ from the reference program's by a relative error of at most 0.0001.
Values sent between devices are 32-bit elements; how exact they have to be, the bound alone decides.
No kernel may reach another device: no remote copies, remote signals or barrier semaphores. Data moves between devices by JAX's collectives and lax.ppermute only.
A program may use at most 64 MiB of HBM per device.

```python
import jax
import jax.numpy as jnp
from jax import lax

CHANNELS = 128
HEIGHT = 32
WIDTH = 32
FACTOR = 4
INTERVALS = 2
LAYERS = 8
SAMPLES = 64


def draw_initial(key, part):
    shape = (SAMPLES, HEIGHT, WIDTH, CHANNELS)
    ramp = 1.0 + 2.0 * jnp.arange(SAMPLES, dtype=jnp.float32) / max(SAMPLES - 1, 1)
    base = jnp.clip(jax.random.normal(key, shape, jnp.float32), -6.0, 6.0)
    return base * ramp[:, None, None, None]


def levels(key, dims, cuts, least, largest):
    def one(axis_at, blocks):
        draws = jax.random.uniform(jax.random.fold_in(jax.random.fold_in(key, 6), axis_at), (blocks,), jnp.float32, least / len(cuts), largest / len(cuts))
        return jnp.repeat(jnp.exp(draws), dims[axis_at] // blocks).reshape((-1,) + (1,) * (len(dims) - axis_at - 1))

    factor_of = one(*cuts[0])
    for cut in cuts[1:]:
        factor_of = factor_of * one(*cut)
    return factor_of


def gaussian(key, shape, deviation, most, shards=(), kind=jnp.bfloat16):
    gain = levels(key, shape, shards, -0.22, 0.18) if shards else 1.0
    drawn = jax.random.normal(key, shape, jnp.float32) * deviation * gain
    return jnp.minimum(jnp.maximum(drawn, -most), most).astype(kind)


def setup_inputs(seed: int = 0) -> dict:
    seeds = jax.random.split(jax.random.key(seed), 5)
    initial = draw_initial(jax.random.fold_in(seeds[4], 71), 0)
    guess = gaussian(seeds[1], (INTERVALS, SAMPLES, HEIGHT, WIDTH, CHANNELS), 1.0, 6.0, ((0, 2), (1, 64)), jnp.float32)
    conv_in = gaussian(seeds[2], (LAYERS, 3, 3, CHANNELS, CHANNELS), (9 * CHANNELS) ** -0.5, 0.1875, ((0, 2),), jnp.float32)
    conv_out = gaussian(seeds[3], (LAYERS, 3, 3, CHANNELS, CHANNELS), (9 * CHANNELS) ** -0.5, 0.1875, ((0, 2),), jnp.float32)
    return dict(initial=initial, guess=guess, conv_in=conv_in, conv_out=conv_out)


EPSILON = 1e-05
STEP_SIZE = 0.25

def convolve(states, kernel):
    return lax.conv_general_dilated(states, kernel, (1, 1), 'SAME', dimension_numbers=('NHWC', 'HWIO', 'NHWC'), precision=lax.Precision.HIGHEST)

def branch(states, kernel_in, kernel_out):
    convolved = convolve(states, kernel_in)
    average = lax.optimization_barrier(jnp.mean(convolved, axis=(0, 1, 2)))
    spread = lax.optimization_barrier(jnp.mean(jnp.square(convolved - average), axis=(0, 1, 2)))
    normed = jax.nn.relu((convolved - average) * lax.rsqrt(spread + EPSILON))
    return convolve(normed, kernel_out)

def sweep(operands):
    start, kernels_in, kernels_out = operands
    current = start
    first = start
    for layer in range(FACTOR):
        current = current + STEP_SIZE * branch(current, kernels_in[layer], kernels_out[layer])
        if layer == 0:
            first = current
    return (current, first)

def reference(initial, guess, conv_in, conv_out):
    kernels_in = conv_in.reshape(INTERVALS, FACTOR, 3, 3, CHANNELS, CHANNELS)
    kernels_out = conv_out.reshape(INTERVALS, FACTOR, 3, 3, CHANNELS, CHANNELS)
    starts = jnp.concatenate([initial[None], guess[:-1]], axis=0)
    ends, unused = lax.map(sweep, (starts, kernels_in, kernels_out))
    restarts = jnp.concatenate([initial[None], ends[:-1]], axis=0)
    fine, first = lax.map(sweep, (restarts, kernels_in, kernels_out))
    tau = fine - (restarts + FACTOR * (first - restarts))

    def coarse(current, operands):
        kernel_in, kernel_out, offset = operands
        following = current + FACTOR * STEP_SIZE * branch(current, kernel_in, kernel_out) + offset
        return (following, following)
    unused_last, corrected = lax.scan(coarse, initial, (kernels_in[:, 0], kernels_out[:, 0], tau))
    return (corrected, ends)
```

```python
import functools

import jax
import jax.numpy as jnp
from jax import lax
from jax.experimental import pallas as pl
from jax.experimental.pallas import tpu as pltpu
from jax.sharding import Mesh
from jax.sharding import PartitionSpec as P

FACTOR = 4
BATCH = ("batch_0", "batch_1", "batch_2")
WORLD = ("depth",) + BATCH

EPSILON = 1e-05
STEP_SIZE = 0.25

ROWS = 32
COLS = 32
CHANNELS = 128
PAIRS = ROWS // 2
CELLS = ROWS * COLS
VMEM_LIMIT = 24 * 2**20


def split(x):
    high = x.astype(jnp.bfloat16)
    low = (x - high.astype(jnp.float32)).astype(jnp.bfloat16)
    return high, low


def place(row, value, high_ref, low_ref):
    at = (row + 1) // 2 * COLS
    lane = 0 if row % 2 else CHANNELS
    high, low = split(value)
    high_ref[at : at + COLS, lane : lane + CHANNELS] = high
    low_ref[at : at + COLS, lane : lane + CHANNELS] = low


def clear_edges(high_ref, low_ref):
    zeros = jnp.zeros((COLS, CHANNELS), jnp.bfloat16)
    for ref in (high_ref, low_ref):
        ref[0:COLS, 0:CHANNELS] = zeros
        ref[PAIRS * COLS : (PAIRS + 1) * COLS, CHANNELS:] = zeros


def convolve(high_ref, low_ref, weights_ref):
    many = PAIRS * COLS
    high0, high1 = high_ref[0:many, :], high_ref[COLS : COLS + many, :]
    low0, low1 = low_ref[0:many, :], low_ref[COLS : COLS + many, :]
    left = jnp.concatenate([high0, high1, low0, low1, high0, high1], axis=1)

    def part(shift):
        high = weights_ref[shift, 0 : 4 * CHANNELS, :]
        low = weights_ref[shift, 4 * CHANNELS : 8 * CHANNELS, :]
        return jnp.dot(
            left, jnp.concatenate([high, high, low], axis=0), preferred_element_type=jnp.float32
        )

    column = lax.broadcasted_iota(jnp.int32, (many, 2 * CHANNELS), 0) % COLS
    out = part(1)
    out = out + jnp.where(column == 0, 0.0, pltpu.roll(part(0), 1, 0))
    return out + jnp.where(column == COLS - 1, 0.0, pltpu.roll(part(2), many - 1, 0))


def pair_rows(out, pair):
    block = out[pair * COLS : (pair + 1) * COLS, :]
    return block[:, :CHANNELS], block[:, CHANNELS:]


def fold(x):
    total = jnp.sum(x, axis=0, keepdims=True)
    return total[:, :CHANNELS] + total[:, CHANNELS:]


def statistics(out):
    total = fold(out)
    own = total * (1.0 / CELLS)
    away = out - jnp.concatenate([own, own], axis=1)
    return total, fold(away * away)


def emit_statistics(out, send_ref, other=None):
    total, square = statistics(out)
    both = jnp.concatenate([total, square], axis=0)
    if other is not None:
        flag, alternative = other
        both = jnp.where(flag == 1, alternative, both)
    send_ref[...] = jnp.broadcast_to(both[None], send_ref.shape)


def combined(received_ref, base):
    rows = received_ref[pl.ds(base, received_ref.shape[0] // 2)]
    samples = rows.shape[0]
    totals = rows[:, 0:1, :]
    average = jnp.sum(totals, axis=0) * (1.0 / (samples * CELLS))
    away = totals * (1.0 / CELLS) - average[None]
    square = jnp.sum(rows[:, 1:2, :], axis=0) + CELLS * jnp.sum(away * away, axis=0)
    return average, lax.rsqrt(square * (1.0 / (samples * CELLS)) + EPSILON)


def normalise(received_ref, base, z_ref, high_ref, low_ref):
    average, factor = combined(received_ref, base)
    for row in range(ROWS):
        place(row, jnp.maximum((z_ref[row] - average) * factor, 0.0), high_ref, low_ref)


def open_kernel(u_ref, win_ref, z_ref, send_ref, high_ref, low_ref):
    clear_edges(high_ref, low_ref)
    for row in range(ROWS):
        place(row, u_ref[row], high_ref, low_ref)
    out = convolve(high_ref, low_ref, win_ref)
    for pair in range(PAIRS):
        z_ref[2 * pair], z_ref[2 * pair + 1] = pair_rows(out, pair)
    emit_statistics(out, send_ref)


def step_kernel(first, mixed, *refs):
    flags_ref, scale_ref, received_ref, z_ref, u_ref, wout_ref, win_ref, *refs = refs
    if mixed:
        other_ref, *refs = refs
    unew_ref, znew_ref, send_ref, *refs = refs
    if first:
        rest_ref, *refs = refs
    high_ref, low_ref = refs
    clear_edges(high_ref, low_ref)
    normalise(received_ref, flags_ref[0], z_ref, high_ref, low_ref)
    out = convolve(high_ref, low_ref, wout_ref)
    scale = scale_ref[0]
    for pair in range(PAIRS):
        for half, block in enumerate(pair_rows(out, pair)):
            row = 2 * pair + half
            before = u_ref[row]
            after = before + scale * block
            unew_ref[row] = after
            place(row, after, high_ref, low_ref)
            if first:
                coarse = before + FACTOR * STEP_SIZE * block
                rest_ref[row] = coarse - (before + FACTOR * (after - before))
    out = convolve(high_ref, low_ref, win_ref)
    for pair in range(PAIRS):
        znew_ref[2 * pair], znew_ref[2 * pair + 1] = pair_rows(out, pair)
    emit_statistics(out, send_ref, (flags_ref[1], other_ref[...]) if mixed else None)


def coarse_kernel(e_ref, rest_ref, win_ref, v_ref, z_ref, stats_ref, high_ref, low_ref):
    clear_edges(high_ref, low_ref)
    for row in range(ROWS):
        value = e_ref[row] + rest_ref[row]
        v_ref[row] = value
        place(row, value, high_ref, low_ref)
    out = convolve(high_ref, low_ref, win_ref)
    for pair in range(PAIRS):
        z_ref[2 * pair], z_ref[2 * pair + 1] = pair_rows(out, pair)
    total, square = statistics(out)
    stats_ref[...] = jnp.concatenate([total, square], axis=0)


def close_kernel(flags_ref, received_ref, z_ref, u_ref, wout_ref, rest_ref, out_ref, high_ref, low_ref):
    first = flags_ref[1] == 1

    @pl.when(first)
    def _():
        out_ref[...] = rest_ref[...]

    @pl.when(jnp.logical_not(first))
    def _():
        clear_edges(high_ref, low_ref)
        normalise(received_ref, flags_ref[0], z_ref, high_ref, low_ref)
        out = convolve(high_ref, low_ref, wout_ref)
        for pair in range(PAIRS):
            for half, block in enumerate(pair_rows(out, pair)):
                row = 2 * pair + half
                out_ref[row] = (u_ref[row] + STEP_SIZE * block) + rest_ref[row]


def prepare_kernel(w_ref, out_ref):
    zeros = jnp.zeros((CHANNELS, CHANNELS), jnp.bfloat16)
    for shift in range(3):
        parts = [split(w_ref[up, shift]) for up in range(3)]
        for kind in range(2):
            w0, w1, w2 = (parts[up][kind] for up in range(3))
            blocks = ((w0, zeros), (w1, w0), (w2, w1), (zeros, w2))
            for at, (one, two) in enumerate(blocks):
                rows = slice((kind * 4 + at) * CHANNELS, (kind * 4 + at + 1) * CHANNELS)
                out_ref[shift, rows, :CHANNELS] = one
                out_ref[shift, rows, CHANNELS:] = two


STATE = jax.ShapeDtypeStruct((ROWS, COLS, CHANNELS), jnp.float32)
PREPARED = jax.ShapeDtypeStruct((3, 8 * CHANNELS, 2 * CHANNELS), jnp.bfloat16)
SMEM = pl.BlockSpec(memory_space=pltpu.SMEM)
VMEM = pl.BlockSpec(memory_space=pltpu.VMEM)
CONV_FLOPS = 2 * 3 * 512 * 1536 * 256


def call(kernel, name, outs, scalars, convs, *args):
    held = [pltpu.VMEM(((PAIRS + 1) * COLS, 2 * CHANNELS), jnp.bfloat16)] * 2
    touched = sum(a.size * a.dtype.itemsize for a in (*args, *outs))
    return pl.pallas_call(
        kernel,
        name=name,
        out_shape=tuple(outs),
        in_specs=[SMEM] * scalars + [VMEM] * (len(args) - scalars),
        out_specs=(VMEM,) * len(outs),
        scratch_shapes=held if convs else [],
        compiler_params=pltpu.CompilerParams(vmem_limit_bytes=VMEM_LIMIT),
        cost_estimate=pl.CostEstimate(
            flops=convs * CONV_FLOPS + 1000, bytes_accessed=touched, transcendentals=0
        ),
    )(*args)


def prepare(weights):
    return call(prepare_kernel, "prepare", (PREPARED,), 0, 0, weights)[0]


def handed(x, pairs):
    return lax.ppermute(x, "depth", pairs)


def exchange(send):
    return lax.all_to_all(send, WORLD, 0, 0)


def body(initial, guess, conv_in, conv_out):
    devices = lax.axis_size(WORLD)
    group = devices // 2
    sent = jax.ShapeDtypeStruct((devices, 2, CHANNELS), jnp.float32)
    small = jax.ShapeDtypeStruct((2, CHANNELS), jnp.float32)
    position = lax.axis_index("depth")
    is_first = position == 0
    flag = is_first.astype(jnp.int32)
    own = jnp.stack([position * group, flag]).astype(jnp.int32)
    of_first = jnp.stack([jnp.zeros_like(position), flag]).astype(jnp.int32)
    fine_scale = jnp.full((1,), STEP_SIZE, jnp.float32)

    onward = [(0, 1)]
    back = [(1, 0)]

    def step(kernel, outs, flags, scale, received, z, u, wout, win, *more):
        return call(
            kernel, "step", outs, 2, 2, flags, scale, received, z, u, wout, win, *more
        )

    plain = functools.partial(step_kernel, False, False)
    before = handed(guess[0, 0], onward)
    start = jnp.where(is_first, initial[0], before)
    z, send = call(open_kernel, "open", (STATE, sent), 0, 1, start, prepare(conv_in[0]))
    received = exchange(send)
    u = start

    next_in = handed(conv_in[0], back)
    next_out = handed(conv_out[0], back)

    u, z, send, rest = step(
        functools.partial(step_kernel, True, False), (STATE, STATE, sent, STATE),
        own, fine_scale, received, z, u, prepare(conv_out[0]), prepare(conv_in[1]),
    )
    received = exchange(send)
    for layer in (1, 2):
        u, z, send = step(
            plain, (STATE, STATE, sent), own, fine_scale, received, z, u,
            prepare(conv_out[layer]), prepare(conv_in[layer + 1]),
        )
        received = exchange(send)
    coarse_in = prepare(next_in)
    ends, z, send = step(
        plain, (STATE, STATE, sent), own, fine_scale, received, z, u,
        prepare(conv_out[3]), coarse_in,
    )
    received = exchange(send)
    t1 = handed(ends, onward)
    zt = handed(z, onward)
    v1, zv, stats = call(
        coarse_kernel, "coarse", (STATE, STATE, small), 0, 1, ends, rest, coarse_in
    )

    a1, z, send = step(
        functools.partial(step_kernel, False, True), (STATE, STATE, sent),
        of_first, fine_scale, received, zt, t1, prepare(conv_out[0]), prepare(conv_in[1]), stats,
    )
    received = exchange(send)
    u = jnp.where(is_first, v1, a1)
    z = jnp.where(is_first, zv, z)
    scale = jnp.where(is_first, FACTOR * STEP_SIZE, STEP_SIZE).reshape(1).astype(jnp.float32)
    u, z, send = step(
        plain, (STATE, STATE, sent), own, scale, received, z, u,
        prepare(jnp.where(is_first, next_out, conv_out[1])), prepare(conv_in[2]),
    )
    received = exchange(send)
    coarse = handed(u, onward)
    rest = jnp.where(is_first, v1, coarse - (t1 + FACTOR * (a1 - t1)))
    u, z, send = step(
        plain, (STATE, STATE, sent), own, fine_scale, received, z, u,
        prepare(conv_out[2]), prepare(conv_in[3]),
    )
    received = exchange(send)
    (result,) = call(
        close_kernel, "close", (STATE,), 1, 1, own, received, z, u, prepare(conv_out[3]), rest
    )
    return (result[None, None], ends[None, None])


def solution(mesh):
    split_mesh = Mesh(
        mesh.devices.reshape(mesh.shape["depth"], 4, 4, 4),
        ("depth", "batch_0", "batch_1", "batch_2"),
    )
    placed = (
        P(BATCH, None, None, None),
        P("depth", BATCH, None, None, None),
        P("depth", None, None, None, None),
        P("depth", None, None, None, None),
    )
    return jax.shard_map(
        body,
        mesh=split_mesh,
        in_specs=placed,
        out_specs=(P("depth", BATCH, None, None, None), P("depth", BATCH, None, None, None)),
        check_vma=False,
    )
```

```python
import functools

import jax
import jax.numpy as jnp
from jax import lax
from jax.experimental import pallas as pl
from jax.experimental.pallas import tpu as pltpu
from jax.sharding import Mesh
from jax.sharding import PartitionSpec as P

FACTOR = 4
BATCH = ("batch_0", "batch_1", "batch_2")
WORLD = ("depth",) + BATCH

EPSILON = 1e-05
STEP_SIZE = 0.25

ROWS = 32
COLS = 32
CHANNELS = 128
PAIRS = ROWS // 2
CELLS = ROWS * COLS
VMEM_LIMIT = 24 * 2**20


def split(x):
    high = x.astype(jnp.bfloat16)
    low = (x - high.astype(jnp.float32)).astype(jnp.bfloat16)
    return high, low


def place(row, value, high_ref, low_ref):
    at = (row + 1) // 2 * COLS
    lane = 0 if row % 2 else CHANNELS
    high, low = split(value)
    high_ref[at : at + COLS, lane : lane + CHANNELS] = high
    low_ref[at : at + COLS, lane : lane + CHANNELS] = low


def clear_edges(high_ref, low_ref):
    zeros = jnp.zeros((COLS, CHANNELS), jnp.bfloat16)
    for ref in (high_ref, low_ref):
        ref[0:COLS, 0:CHANNELS] = zeros
        ref[PAIRS * COLS : (PAIRS + 1) * COLS, CHANNELS:] = zeros


def convolve(high_ref, low_ref, weights):
    many = PAIRS * COLS
    high0, high1 = high_ref[0:many, :], high_ref[COLS : COLS + many, :]
    low0, low1 = low_ref[0:many, :], low_ref[COLS : COLS + many, :]
    left = jnp.concatenate([high0, high1, low0, low1, high0, high1], axis=1)
    zeros = jnp.zeros((CHANNELS, CHANNELS), jnp.bfloat16)

    def part(shift):
        rows = []
        for kind in range(2):
            w0, w1, w2 = (weights[kind, up, shift] for up in range(3))
            blocks = ((w0, zeros), (w1, w0), (w2, w1), (zeros, w2))
            rows.append([jnp.concatenate(b, axis=1) for b in blocks])
        right = jnp.concatenate(rows[0] + rows[0] + rows[1], axis=0)
        return jnp.dot(left, right, preferred_element_type=jnp.float32)

    column = lax.broadcasted_iota(jnp.int32, (many, 2 * CHANNELS), 0) % COLS
    out = part(1)
    out = out + jnp.where(column == 0, 0.0, pltpu.roll(part(0), 1, 0))
    return out + jnp.where(column == COLS - 1, 0.0, pltpu.roll(part(2), many - 1, 0))


def pair_rows(out, pair):
    block = out[pair * COLS : (pair + 1) * COLS, :]
    return block[:, :CHANNELS], block[:, CHANNELS:]


def fold(x):
    total = jnp.sum(x, axis=0, keepdims=True)
    return total[:, :CHANNELS] + total[:, CHANNELS:]


def statistics(out):
    total = fold(out)
    own = total * (1.0 / CELLS)
    away = out - jnp.concatenate([own, own], axis=1)
    return total, fold(away * away)


def emit_statistics(out, send_ref):
    both = jnp.concatenate(statistics(out), axis=0)
    send_ref[...] = jnp.broadcast_to(both[None], send_ref.shape)


def combined(received_ref, base):
    rows = received_ref[pl.ds(base, received_ref.shape[0] // 2)]
    samples = rows.shape[0]
    totals = rows[:, 0:1, :]
    average = jnp.sum(totals, axis=0) * (1.0 / (samples * CELLS))
    away = totals * (1.0 / CELLS) - average[None]
    square = jnp.sum(rows[:, 1:2, :], axis=0) + CELLS * jnp.sum(away * away, axis=0)
    return average, lax.rsqrt(square * (1.0 / (samples * CELLS)) + EPSILON)


def normalise(received_ref, base, z_ref, held):
    average, factor = combined(received_ref, base)
    clear_edges(*held)
    for row in range(ROWS):
        place(row, jnp.maximum((z_ref[row] - average) * factor, 0.0), *held)


def into_conv(held, weights, z_ref, send_ref):
    out = convolve(*held, weights)
    for pair in range(PAIRS):
        z_ref[2 * pair], z_ref[2 * pair + 1] = pair_rows(out, pair)
    emit_statistics(out, send_ref)


def branch_blocks(held, weights):
    out = convolve(*held, weights)
    for pair in range(PAIRS):
        for half, block in enumerate(pair_rows(out, pair)):
            yield 2 * pair + half, block


def add_branch(held, weights, scale, u_ref, unew_ref, again=True):
    for row, block in branch_blocks(held, weights):
        after = u_ref[row] + scale * block
        unew_ref[row] = after
        if again:
            place(row, after, *held)


def load_kernel(layers, flags_ref, in_hbm, out_hbm, in_ref, out_ref, packed_ref, raw_ref, sem):
    jobs = [(which, layer) for layer in range(layers) for which in range(2)]
    sources, targets = (in_hbm, out_hbm), (in_ref, out_ref)
    copies = [
        pltpu.make_async_copy(sources[which].at[layer], raw_ref.at[at], sem.at[at])
        for at, (which, layer) in enumerate(jobs)
    ]
    for copy in copies:
        copy.start()
    for at, (which, layer) in enumerate(jobs):
        copies[at].wait()
        for up in range(3):
            for across in range(3):
                value = raw_ref[at, up, across]
                high, low = split(value)
                targets[which][layer, 0, up, across] = high
                targets[which][layer, 1, up, across] = low
                if layer == 0:
                    packed_ref[which, up, across] = value


def split_weights(raw_ref, which, weights_ref):
    for up in range(3):
        for across in range(3):
            high, low = split(raw_ref[which, up, across])
            weights_ref[0, up, across] = high
            weights_ref[1, up, across] = low


def open_kernel(flags_ref, initial_ref, before_ref, win_ref, z_ref, u_ref, send_ref, *held):
    @pl.when(flags_ref[1] == 1)
    def _():
        u_ref[...] = initial_ref[...]

    @pl.when(flags_ref[1] == 0)
    def _():
        u_ref[...] = before_ref[...]

    clear_edges(*held)
    for row in range(ROWS):
        place(row, u_ref[row], *held)
    into_conv(held, win_ref.at[0], z_ref, send_ref)


def step_kernel(
    layer, flags_ref, received_ref, z_ref, u_ref, wout_ref, win_ref, unew_ref, znew_ref, send_ref, *refs
):
    *rest_ref, high_ref, low_ref = refs
    held = (high_ref, low_ref)
    normalise(received_ref, flags_ref[0], z_ref, held)
    if layer == 0:
        (rest_ref,) = rest_ref
        for row, block in branch_blocks(held, wout_ref.at[layer]):
            before = u_ref[row]
            after = before + STEP_SIZE * block
            unew_ref[row] = after
            place(row, after, *held)
            coarse = before + FACTOR * STEP_SIZE * block
            rest_ref[row] = coarse - (before + FACTOR * (after - before))
    else:
        add_branch(held, wout_ref.at[layer], STEP_SIZE, u_ref, unew_ref)
    into_conv(held, win_ref.at[layer + 1], znew_ref, send_ref)


def turn_kernel(
    flags_ref, received_ref, z_ref, u_ref, wout_ref, moved_ref, both_ref, ends_ref, send_ref, high_ref, low_ref, weights_ref
):
    held = (high_ref, low_ref)
    normalise(received_ref, flags_ref[0], z_ref, held)
    for row, block in branch_blocks(held, wout_ref.at[FACTOR - 1]):
        after = u_ref[row] + STEP_SIZE * block
        both_ref[0, row] = after
        ends_ref[row] = after
        place(row, after, *held)

    @pl.when(flags_ref[1] == 1)
    def _():
        split_weights(moved_ref, 0, weights_ref)
        into_conv(held, weights_ref, both_ref.at[1], send_ref)


def fork_kernel(
    flags_ref, received_ref, arrived_ref, both_ref, rest_ref, wout_ref, win_ref, moved_ref,
    unew_ref, znew_ref, send_ref, high_ref, low_ref, weights_ref,
):
    held = (high_ref, low_ref)

    @pl.when(flags_ref[1] == 1)
    def _():
        clear_edges(*held)
        for row in range(ROWS):
            value = both_ref[0, row] + rest_ref[row]
            unew_ref[row] = value
            place(row, value, *held)
        split_weights(moved_ref, 0, weights_ref)
        into_conv(held, weights_ref, znew_ref, send_ref)

    @pl.when(flags_ref[1] == 0)
    def _():
        normalise(received_ref, 0, arrived_ref.at[1], held)
        add_branch(held, wout_ref.at[0], STEP_SIZE, arrived_ref.at[0], unew_ref)
        into_conv(held, win_ref.at[1], znew_ref, send_ref)


def coarse_kernel(
    flags_ref, received_ref, z_ref, u_ref, wout_ref, win_ref, moved_ref,
    unew_ref, znew_ref, send_ref, high_ref, low_ref, weights_ref,
):
    held = (high_ref, low_ref)
    normalise(received_ref, flags_ref[0], z_ref, held)

    @pl.when(flags_ref[1] == 1)
    def _():
        split_weights(moved_ref, 1, weights_ref)
        add_branch(held, weights_ref, FACTOR * STEP_SIZE, u_ref, unew_ref, again=False)

    @pl.when(flags_ref[1] == 0)
    def _():
        add_branch(held, wout_ref.at[1], STEP_SIZE, u_ref, unew_ref)
        into_conv(held, win_ref.at[2], znew_ref, send_ref)


def second_kernel(flags_ref, *refs):
    @pl.when(flags_ref[1] == 0)
    def _():
        step_kernel(2, flags_ref, *refs)


def close_kernel(
    flags_ref, received_ref, z_ref, u_ref, wout_ref, arrived_ref, first_ref, coarse_ref, out_ref, *held
):
    @pl.when(flags_ref[1] == 1)
    def _():
        out_ref[...] = first_ref[...]

    @pl.when(flags_ref[1] == 0)
    def _():
        normalise(received_ref, flags_ref[0], z_ref, held)
        for row, block in branch_blocks(held, wout_ref.at[FACTOR - 1]):
            fine = u_ref[row] + STEP_SIZE * block
            begun, first = arrived_ref[0, row], first_ref[row]
            tau = fine - (begun + FACTOR * (first - begun))
            out_ref[row] = coarse_ref[row] + tau


STATE = jax.ShapeDtypeStruct((ROWS, COLS, CHANNELS), jnp.float32)
BOTH = jax.ShapeDtypeStruct((2, ROWS, COLS, CHANNELS), jnp.float32)
SMEM = pl.BlockSpec(memory_space=pltpu.SMEM)
VMEM = pl.BlockSpec(memory_space=pltpu.VMEM)
HELD = [pltpu.VMEM(((PAIRS + 1) * COLS, 2 * CHANNELS), jnp.bfloat16)] * 2
WEIGHTS = [pltpu.VMEM((2, 3, 3, CHANNELS, CHANNELS), jnp.bfloat16)]
CONV_FLOPS = 2 * 3 * 512 * 1536 * 256


def call(kernel, name, outs, convs, scratch, *args):
    touched = sum(a.size * a.dtype.itemsize for a in (*args, *outs))
    return pl.pallas_call(
        kernel,
        name=name,
        out_shape=tuple(outs),
        in_specs=[SMEM] + [VMEM] * (len(args) - 1),
        out_specs=(VMEM,) * len(outs),
        scratch_shapes=scratch,
        compiler_params=pltpu.CompilerParams(vmem_limit_bytes=VMEM_LIMIT),
        cost_estimate=pl.CostEstimate(
            flops=convs * CONV_FLOPS, bytes_accessed=touched, transcendentals=0
        ),
    )(*args)


def load(flags, conv_in, conv_out):
    layers = conv_in.shape[0]
    shape = conv_in.shape[1:]
    ready = jax.ShapeDtypeStruct((layers, 2) + shape, jnp.bfloat16)
    packed = jax.ShapeDtypeStruct((2,) + shape, jnp.float32)
    return pl.pallas_call(
        functools.partial(load_kernel, layers),
        name="load",
        out_shape=(ready, ready, packed),
        in_specs=[SMEM] + [pl.BlockSpec(memory_space=pltpu.HBM)] * 2,
        out_specs=(VMEM,) * 3,
        scratch_shapes=[
            pltpu.VMEM((2 * layers,) + shape, jnp.float32),
            pltpu.SemaphoreType.DMA((2 * layers,)),
        ],
        compiler_params=pltpu.CompilerParams(vmem_limit_bytes=VMEM_LIMIT),
        cost_estimate=pl.CostEstimate(
            flops=1000, bytes_accessed=4 * conv_in.size * 4, transcendentals=0
        ),
    )(flags, conv_in, conv_out)


def handed(x, pairs):
    return lax.ppermute(x, "depth", pairs)


def exchange(send):
    return lax.all_to_all(send, WORLD, 0, 0)


def body(initial, guess, conv_in, conv_out):
    devices = lax.axis_size(WORLD)
    sent = jax.ShapeDtypeStruct((devices, 2, CHANNELS), jnp.float32)
    position = lax.axis_index("depth")
    flags = jnp.stack([position * (devices // 2), 1 - position]).astype(jnp.int32)
    outs = (STATE, STATE, sent)

    before = handed(guess[0, 0], [(0, 1)])
    ready_in, ready_out, packed = load(flags, conv_in, conv_out)
    moved = handed(packed, [(1, 0)])
    z, u, send = call(open_kernel, "open", outs, 1, HELD, flags, initial[0], before, ready_in)
    send, moved = lax.optimization_barrier((send, moved))
    received = exchange(send)
    u, z, send, rest = call(
        functools.partial(step_kernel, 0), "step", outs + (STATE,), 2, HELD,
        flags, received, z, u, ready_out, ready_in,
    )
    received = exchange(send)
    for layer in (1, 2):
        u, z, send = call(
            functools.partial(step_kernel, layer), "step", outs, 2, HELD,
            flags, received, z, u, ready_out, ready_in,
        )
        received = exchange(send)
    both, ends, send = call(
        turn_kernel, "turn", (BOTH, STATE, sent), 2, HELD + WEIGHTS,
        flags, received, z, u, ready_out, moved,
    )
    arrived = handed(both, [(0, 1)])
    received = exchange(send)
    first, z, send = call(
        fork_kernel, "fork", outs, 2, HELD + WEIGHTS,
        flags, received, arrived, both, rest, ready_out, ready_in, moved,
    )
    received = exchange(send)
    u, z, send = call(
        coarse_kernel, "coarse", outs, 2, HELD + WEIGHTS,
        flags, received, z, first, ready_out, ready_in, moved,
    )
    coarse = handed(u, [(0, 1)])
    received = exchange(send)
    u, z, send = call(
        second_kernel, "second", outs, 2, HELD, flags, received, z, u, ready_out, ready_in
    )
    received = exchange(send)
    (result,) = call(
        close_kernel, "close", (STATE,), 1, HELD,
        flags, received, z, u, ready_out, arrived, first, coarse,
    )
    return (result[None, None], ends[None, None])


def solution(mesh):
    split_mesh = Mesh(
        mesh.devices.reshape(mesh.shape["depth"], 4, 4, 4),
        ("depth", "batch_0", "batch_1", "batch_2"),
    )
    placed = (
        P(BATCH, None, None, None),
        P("depth", BATCH, None, None, None),
        P("depth", None, None, None, None),
        P("depth", None, None, None, None),
    )
    return jax.shard_map(
        body,
        mesh=split_mesh,
        in_specs=placed,
        out_specs=(P("depth", BATCH, None, None, None), P("depth", BATCH, None, None, None)),
        check_vma=False,
    )
```

```python
import functools

import jax
import jax.numpy as jnp
from jax import lax
from jax.experimental import pallas as pl
from jax.experimental.pallas import tpu as pltpu
from jax.sharding import Mesh
from jax.sharding import PartitionSpec as P

FACTOR = 4
BATCH = ("batch_0", "batch_1", "batch_2")
WORLD = ("depth",) + BATCH

EPSILON = 1e-05
STEP_SIZE = 0.25

ROWS = 32
COLS = 32
CHANNELS = 128
PAIRS = ROWS // 2
CELLS = ROWS * COLS
VMEM_LIMIT = 24 * 2**20
READY_LIMIT = 24 * 2**20


def split(x):
    high = x.astype(jnp.bfloat16)
    low = (x - high.astype(jnp.float32)).astype(jnp.bfloat16)
    return high, low


def place(row, value, high_ref, low_ref):
    at = (row + 1) // 2 * COLS
    lane = 0 if row % 2 else CHANNELS
    high, low = split(value)
    high_ref[at : at + COLS, lane : lane + CHANNELS] = high
    low_ref[at : at + COLS, lane : lane + CHANNELS] = low


def clear_edges(high_ref, low_ref):
    zeros = jnp.zeros((COLS, CHANNELS), jnp.bfloat16)
    for ref in (high_ref, low_ref):
        ref[0:COLS, 0:CHANNELS] = zeros
        ref[PAIRS * COLS : (PAIRS + 1) * COLS, CHANNELS:] = zeros


def convolve(high_ref, low_ref, weights):
    many = PAIRS * COLS
    high0, high1 = high_ref[0:many, :], high_ref[COLS : COLS + many, :]
    low0, low1 = low_ref[0:many, :], low_ref[COLS : COLS + many, :]
    left = jnp.concatenate([high0, high1, low0, low1, high0, high1], axis=1)
    zeros = jnp.zeros((CHANNELS, CHANNELS), jnp.bfloat16)

    def part(shift):
        rows = []
        for kind in range(2):
            w0, w1, w2 = (weights[kind, up, shift] for up in range(3))
            blocks = ((w0, zeros), (w1, w0), (w2, w1), (zeros, w2))
            rows.append([jnp.concatenate(b, axis=1) for b in blocks])
        right = jnp.concatenate(rows[0] + rows[0] + rows[1], axis=0)
        return jnp.dot(left, right, preferred_element_type=jnp.float32)

    column = lax.broadcasted_iota(jnp.int32, (many, 2 * CHANNELS), 0) % COLS
    out = part(1)
    out = out + jnp.where(column == 0, 0.0, pltpu.roll(part(0), 1, 0))
    return out + jnp.where(column == COLS - 1, 0.0, pltpu.roll(part(2), many - 1, 0))


def pair_rows(out, pair):
    block = out[pair * COLS : (pair + 1) * COLS, :]
    return block[:, :CHANNELS], block[:, CHANNELS:]


def fold(x):
    total = jnp.sum(x, axis=0, keepdims=True)
    return total[:, :CHANNELS] + total[:, CHANNELS:]


def statistics(out):
    total = fold(out)
    own = total * (1.0 / CELLS)
    away = out - jnp.concatenate([own, own], axis=1)
    return total, fold(away * away)


def emit_statistics(out, send_ref):
    both = jnp.concatenate(statistics(out), axis=0)
    send_ref[...] = jnp.broadcast_to(both[None], send_ref.shape)


def combined(received_ref, base):
    rows = received_ref[pl.ds(base, received_ref.shape[0] // 2)]
    samples = rows.shape[0]
    totals = rows[:, 0:1, :]
    average = jnp.sum(totals, axis=0) * (1.0 / (samples * CELLS))
    away = totals * (1.0 / CELLS) - average[None]
    square = jnp.sum(rows[:, 1:2, :], axis=0) + CELLS * jnp.sum(away * away, axis=0)
    return average, lax.rsqrt(square * (1.0 / (samples * CELLS)) + EPSILON)


def normalise(received_ref, base, z_ref, held):
    average, factor = combined(received_ref, base)
    clear_edges(*held)
    for row in range(ROWS):
        place(row, jnp.maximum((z_ref[row] - average) * factor, 0.0), *held)


def into_conv(held, weights, z_ref, send_ref):
    out = convolve(*held, weights)
    for pair in range(PAIRS):
        z_ref[2 * pair], z_ref[2 * pair + 1] = pair_rows(out, pair)
    emit_statistics(out, send_ref)


def branch_blocks(held, weights):
    out = convolve(*held, weights)
    for pair in range(PAIRS):
        for half, block in enumerate(pair_rows(out, pair)):
            yield 2 * pair + half, block


def add_branch(held, weights, scale, u_ref, unew_ref, again=True):
    for row, block in branch_blocks(held, weights):
        after = u_ref[row] + scale * block
        unew_ref[row] = after
        if again:
            place(row, after, *held)


def split_weights(raw_ref, at, weights_ref):
    for up in range(3):
        for across in range(3):
            high, low = split(raw_ref[at, up, across])
            weights_ref[0, up, across] = high
            weights_ref[1, up, across] = low


def ready_kernel(flags_ref, initial_hbm, win_hbm, initial_ref, weights_ref, raw_ref, sem):
    weights = pltpu.make_async_copy(win_hbm.at[pl.ds(0, 1)], raw_ref, sem.at[0])
    state = pltpu.make_async_copy(initial_hbm, initial_ref, sem.at[1])
    weights.start()
    state.start()
    weights.wait()
    split_weights(raw_ref, 0, weights_ref)
    state.wait()


def open_kernel(flags_ref, initial_ref, before_ref, weights_ref, z_ref, u_ref, send_ref, *held):
    @pl.when(flags_ref[1] == 1)
    def _():
        u_ref[...] = initial_ref[...]

    @pl.when(flags_ref[1] == 0)
    def _():
        u_ref[...] = before_ref[...]

    clear_edges(*held)
    for row in range(ROWS):
        place(row, u_ref[row], *held)
    into_conv(held, weights_ref, z_ref, send_ref)


def step_kernel(
    layer, flags_ref, received_ref, z_ref, u_ref, wout_ref, win_ref, unew_ref, znew_ref, send_ref, *refs
):
    *more, high_ref, low_ref, ending_ref, begun_ref = refs
    held = (high_ref, low_ref)
    split_weights(wout_ref, layer, ending_ref)
    normalise(received_ref, flags_ref[0], z_ref, held)
    if layer == 0:
        rest_ref, packed_ref = more
        packed_ref[0] = win_ref[0]
        packed_ref[1] = wout_ref[0]
        for row, block in branch_blocks(held, ending_ref):
            before = u_ref[row]
            after = before + STEP_SIZE * block
            unew_ref[row] = after
            place(row, after, *held)
            coarse = before + FACTOR * STEP_SIZE * block
            rest_ref[row] = coarse - (before + FACTOR * (after - before))
    else:
        add_branch(held, ending_ref, STEP_SIZE, u_ref, unew_ref)
    split_weights(win_ref, layer + 1, begun_ref)
    into_conv(held, begun_ref, znew_ref, send_ref)


def turn_kernel(
    flags_ref, received_ref, z_ref, u_ref, wout_ref, moved_ref, both_ref, ends_ref, send_ref, high_ref, low_ref, ending_ref, weights_ref
):
    held = (high_ref, low_ref)
    split_weights(wout_ref, FACTOR - 1, ending_ref)
    normalise(received_ref, flags_ref[0], z_ref, held)
    for row, block in branch_blocks(held, ending_ref):
        after = u_ref[row] + STEP_SIZE * block
        both_ref[0, row] = after
        ends_ref[row] = after
        place(row, after, *held)

    @pl.when(flags_ref[1] == 1)
    def _():
        split_weights(moved_ref, 0, weights_ref)
        into_conv(held, weights_ref, both_ref.at[1], send_ref)


def fork_kernel(
    flags_ref, received_ref, arrived_ref, both_ref, rest_ref, wout_ref, win_ref, moved_ref,
    unew_ref, znew_ref, send_ref, high_ref, low_ref, ending_ref, weights_ref,
):
    held = (high_ref, low_ref)

    @pl.when(flags_ref[1] == 1)
    def _():
        clear_edges(*held)
        for row in range(ROWS):
            value = both_ref[0, row] + rest_ref[row]
            unew_ref[row] = value
            place(row, value, *held)
        split_weights(moved_ref, 0, weights_ref)
        into_conv(held, weights_ref, znew_ref, send_ref)

    @pl.when(flags_ref[1] == 0)
    def _():
        split_weights(wout_ref, 0, ending_ref)
        normalise(received_ref, 0, arrived_ref.at[1], held)
        add_branch(held, ending_ref, STEP_SIZE, arrived_ref.at[0], unew_ref)
        split_weights(win_ref, 1, weights_ref)
        into_conv(held, weights_ref, znew_ref, send_ref)


def coarse_kernel(
    flags_ref, received_ref, z_ref, u_ref, wout_ref, win_ref, moved_ref,
    unew_ref, znew_ref, send_ref, high_ref, low_ref, ending_ref, weights_ref,
):
    held = (high_ref, low_ref)
    normalise(received_ref, flags_ref[0], z_ref, held)

    @pl.when(flags_ref[1] == 1)
    def _():
        split_weights(moved_ref, 1, weights_ref)
        add_branch(held, weights_ref, FACTOR * STEP_SIZE, u_ref, unew_ref, again=False)

    @pl.when(flags_ref[1] == 0)
    def _():
        split_weights(wout_ref, 1, ending_ref)
        add_branch(held, ending_ref, STEP_SIZE, u_ref, unew_ref)
        split_weights(win_ref, 2, weights_ref)
        into_conv(held, weights_ref, znew_ref, send_ref)


def second_kernel(flags_ref, *refs):
    @pl.when(flags_ref[1] == 0)
    def _():
        step_kernel(2, flags_ref, *refs)


def close_kernel(
    flags_ref, received_ref, z_ref, u_ref, wout_ref, arrived_ref, first_ref, coarse_ref, out_ref, *held
):
    @pl.when(flags_ref[1] == 1)
    def _():
        out_ref[...] = first_ref[...]

    @pl.when(flags_ref[1] == 0)
    def _():
        *states, weights_ref = held
        split_weights(wout_ref, FACTOR - 1, weights_ref)
        normalise(received_ref, flags_ref[0], z_ref, states)
        for row, block in branch_blocks(states, weights_ref):
            fine = u_ref[row] + STEP_SIZE * block
            begun, first = arrived_ref[0, row], first_ref[row]
            tau = fine - (begun + FACTOR * (first - begun))
            out_ref[row] = coarse_ref[row] + tau


STATE = jax.ShapeDtypeStruct((ROWS, COLS, CHANNELS), jnp.float32)
BOTH = jax.ShapeDtypeStruct((2, ROWS, COLS, CHANNELS), jnp.float32)
SMEM = pl.BlockSpec(memory_space=pltpu.SMEM)
VMEM = pl.BlockSpec(memory_space=pltpu.VMEM)
HELD = [pltpu.VMEM(((PAIRS + 1) * COLS, 2 * CHANNELS), jnp.bfloat16)] * 2
WEIGHTS = [pltpu.VMEM((2, 3, 3, CHANNELS, CHANNELS), jnp.bfloat16)]
ONE = HELD + WEIGHTS
TWO = HELD + WEIGHTS * 2
CONV_FLOPS = 2 * 3 * 512 * 1536 * 256


def call(kernel, name, outs, convs, scratch, *args):
    touched = sum(a.size * a.dtype.itemsize for a in (*args, *outs))
    return pl.pallas_call(
        kernel,
        name=name,
        out_shape=tuple(outs),
        in_specs=[SMEM] + [VMEM] * (len(args) - 1),
        out_specs=(VMEM,) * len(outs),
        scratch_shapes=scratch,
        compiler_params=pltpu.CompilerParams(vmem_limit_bytes=VMEM_LIMIT),
        cost_estimate=pl.CostEstimate(
            flops=convs * CONV_FLOPS, bytes_accessed=touched, transcendentals=0
        ),
    )(*args)


def ready(flags, initial, conv_in):
    shape = conv_in.shape[1:]
    return pl.pallas_call(
        ready_kernel,
        name="ready",
        out_shape=(STATE, jax.ShapeDtypeStruct((2,) + shape, jnp.bfloat16)),
        in_specs=[SMEM] + [pl.BlockSpec(memory_space=pltpu.HBM)] * 2,
        out_specs=(VMEM,) * 2,
        scratch_shapes=[
            pltpu.VMEM((1,) + shape, jnp.float32),
            pltpu.SemaphoreType.DMA((2,)),
        ],
        compiler_params=pltpu.CompilerParams(vmem_limit_bytes=READY_LIMIT),
        cost_estimate=pl.CostEstimate(flops=1000, bytes_accessed=3000000, transcendentals=0),
    )(flags, *(pltpu.with_memory_space_constraint(x, pltpu.HBM) for x in (initial, conv_in)))


def swapped(x):
    return lax.ppermute(x, "depth", [(0, 1), (1, 0)])


def exchange(send):
    return lax.all_to_all(send, WORLD, 0, 0)


def body(initial, guess, conv_in, conv_out):
    devices = lax.axis_size(WORLD)
    sent = jax.ShapeDtypeStruct((devices, 2, CHANNELS), jnp.float32)
    position = lax.axis_index("depth")
    flags = jnp.stack([position * (devices // 2), 1 - position]).astype(jnp.int32)
    outs = (STATE, STATE, sent)

    before = swapped(guess[0, 0])
    held, weights = ready(flags, initial[0], conv_in)
    z, u, send = call(open_kernel, "open", outs, 1, HELD, flags, held, before, weights)
    received = exchange(send)
    packed = jax.ShapeDtypeStruct((2,) + conv_in.shape[1:], jnp.float32)
    u, z, send, rest, packed = call(
        functools.partial(step_kernel, 0), "step", outs + (STATE, packed), 2, TWO,
        flags, received, z, u, conv_out, conv_in,
    )
    moved = swapped(packed)
    received = exchange(send)
    for layer in (1, 2):
        u, z, send = call(
            functools.partial(step_kernel, layer), "step", outs, 2, TWO,
            flags, received, z, u, conv_out, conv_in,
        )
        received = exchange(send)
    both, ends, send = call(
        turn_kernel, "turn", (BOTH, STATE, sent), 2, TWO,
        flags, received, z, u, conv_out, moved,
    )
    arrived = swapped(both)
    received = exchange(send)
    first, z, send = call(
        fork_kernel, "fork", outs, 2, TWO,
        flags, received, arrived, both, rest, conv_out, conv_in, moved,
    )
    received = exchange(send)
    u, z, send = call(
        coarse_kernel, "coarse", outs, 2, TWO,
        flags, received, z, first, conv_out, conv_in, moved,
    )
    coarse = swapped(u)
    received = exchange(send)
    u, z, send = call(
        second_kernel, "second", outs, 2, TWO, flags, received, z, u, conv_out, conv_in
    )
    received = exchange(send)
    (result,) = call(
        close_kernel, "close", (STATE,), 1, ONE,
        flags, received, z, u, conv_out, arrived, first, coarse,
    )
    return (result[None, None], ends[None, None])


def solution(mesh):
    split_mesh = Mesh(
        mesh.devices.reshape(mesh.shape["depth"], 4, 4, 4),
        ("depth", "batch_0", "batch_1", "batch_2"),
    )
    placed = (
        P(BATCH, None, None, None),
        P("depth", BATCH, None, None, None),
        P("depth", None, None, None, None),
        P("depth", None, None, None, None),
    )
    return jax.shard_map(
        body,
        mesh=split_mesh,
        in_specs=placed,
        out_specs=(P("depth", BATCH, None, None, None), P("depth", BATCH, None, None, None)),
        check_vma=False,
    )
```

```python
import functools

import jax
import jax.numpy as jnp
from jax import lax
from jax.experimental import pallas as pl
from jax.experimental.pallas import tpu as pltpu
from jax.sharding import Mesh
from jax.sharding import PartitionSpec as P

FACTOR = 4
BATCH = ("batch_0", "batch_1", "batch_2")
WORLD = ("depth",) + BATCH

EPSILON = 1e-05
STEP_SIZE = 0.25

ROWS = 32
COLS = 32
CHANNELS = 128
PAIRS = ROWS // 2
CELLS = ROWS * COLS
CHUNKS = 2
PART = PAIRS // CHUNKS
VMEM_LIMIT = 24 * 2**20
READY_LIMIT = 24 * 2**20


def split(x):
    high = x.astype(jnp.bfloat16)
    low = (x - high.astype(jnp.float32)).astype(jnp.bfloat16)
    return high, low


def place(row, value, high_ref, low_ref):
    at = (row + 1) // 2 * COLS
    lane = 0 if row % 2 else CHANNELS
    high, low = split(value)
    high_ref[at : at + COLS, lane : lane + CHANNELS] = high
    low_ref[at : at + COLS, lane : lane + CHANNELS] = low


def clear_edges(high_ref, low_ref):
    zeros = jnp.zeros((COLS, CHANNELS), jnp.bfloat16)
    for ref in (high_ref, low_ref):
        ref[0:COLS, 0:CHANNELS] = zeros
        ref[PAIRS * COLS : (PAIRS + 1) * COLS, CHANNELS:] = zeros


def convolve(high_ref, low_ref, weights, chunk):
    many = PART * COLS
    at = chunk * many
    high0, high1 = high_ref[at : at + many, :], high_ref[at + COLS : at + COLS + many, :]
    low0, low1 = low_ref[at : at + many, :], low_ref[at + COLS : at + COLS + many, :]
    left = jnp.concatenate([high0, high1, low0, low1, high0, high1], axis=1)
    zeros = jnp.zeros((CHANNELS, CHANNELS), jnp.bfloat16)

    def part(shift):
        rows = []
        for kind in range(2):
            w0, w1, w2 = (weights[kind, up, shift] for up in range(3))
            blocks = ((w0, zeros), (w1, w0), (w2, w1), (zeros, w2))
            rows.append([jnp.concatenate(b, axis=1) for b in blocks])
        right = jnp.concatenate(rows[0] + rows[0] + rows[1], axis=0)
        return jnp.dot(left, right, preferred_element_type=jnp.float32)

    column = lax.broadcasted_iota(jnp.int32, (many, 2 * CHANNELS), 0) % COLS
    out = part(1)
    out = out + jnp.where(column == 0, 0.0, pltpu.roll(part(0), 1, 0))
    return out + jnp.where(column == COLS - 1, 0.0, pltpu.roll(part(2), many - 1, 0))


def branch_blocks(held, weights):
    for chunk in range(CHUNKS):
        out = convolve(*held, weights, chunk)
        for pair in range(PART):
            block = out[pair * COLS : (pair + 1) * COLS, :]
            row = 2 * (chunk * PART + pair)
            yield row, block[:, :CHANNELS]
            yield row + 1, block[:, CHANNELS:]


def into_conv(held, weights, z_ref, send_ref):
    totals, squares = [], []
    for chunk in range(CHUNKS):
        out = convolve(*held, weights, chunk)
        for pair in range(PART):
            block = out[pair * COLS : (pair + 1) * COLS, :]
            row = 2 * (chunk * PART + pair)
            z_ref[row], z_ref[row + 1] = block[:, :CHANNELS], block[:, CHANNELS:]
        total = jnp.sum(out, axis=0, keepdims=True)
        away = out - total * (1.0 / (PART * COLS))
        square = jnp.sum(away * away, axis=0, keepdims=True)
        for half in range(2):
            totals.append(total[:, half * CHANNELS : (half + 1) * CHANNELS])
            squares.append(square[:, half * CHANNELS : (half + 1) * CHANNELS])
    total = functools.reduce(jnp.add, totals)
    square = functools.reduce(jnp.add, squares)
    for part in totals:
        away = part * (1.0 / (PART * COLS)) - total * (1.0 / CELLS)
        square = square + (PART * COLS) * (away * away)
    both = jnp.concatenate([total, square], axis=0)
    send_ref[...] = jnp.broadcast_to(both[None], send_ref.shape)


def combined(received_ref, base):
    rows = received_ref[pl.ds(base, received_ref.shape[0] // 2)]
    samples = rows.shape[0]
    totals = rows[:, 0:1, :]
    average = jnp.sum(totals, axis=0) * (1.0 / (samples * CELLS))
    away = totals * (1.0 / CELLS) - average[None]
    square = jnp.sum(rows[:, 1:2, :], axis=0) + CELLS * jnp.sum(away * away, axis=0)
    return average, lax.rsqrt(square * (1.0 / (samples * CELLS)) + EPSILON)


def normalise(received_ref, base, z_ref, held):
    average, factor = combined(received_ref, base)
    clear_edges(*held)
    for row in range(ROWS):
        place(row, jnp.maximum((z_ref[row] - average) * factor, 0.0), *held)


def add_branch(held, weights, scale, u_ref, unew_ref, onto=None):
    if onto is not None:
        clear_edges(*onto)
    for row, block in branch_blocks(held, weights):
        after = u_ref[row] + scale * block
        unew_ref[row] = after
        if onto is not None:
            place(row, after, *onto)


def split_weights(raw_ref, at, weights_ref):
    for up in range(3):
        for across in range(3):
            high, low = split(raw_ref[at, up, across])
            weights_ref[0, up, across] = high
            weights_ref[1, up, across] = low


def ready_kernel(flags_ref, initial_hbm, win_hbm, initial_ref, weights_ref, raw_ref, sem):
    weights = pltpu.make_async_copy(win_hbm.at[pl.ds(0, 1)], raw_ref, sem.at[0])
    state = pltpu.make_async_copy(initial_hbm, initial_ref, sem.at[1])
    weights.start()
    state.start()
    weights.wait()
    split_weights(raw_ref, 0, weights_ref)
    state.wait()


def open_kernel(flags_ref, initial_ref, before_ref, weights_ref, z_ref, u_ref, send_ref, *held):
    @pl.when(flags_ref[1] == 1)
    def _():
        u_ref[...] = initial_ref[...]

    @pl.when(flags_ref[1] == 0)
    def _():
        u_ref[...] = before_ref[...]

    clear_edges(*held)
    for row in range(ROWS):
        place(row, u_ref[row], *held)
    into_conv(held, weights_ref, z_ref, send_ref)


def step_kernel(
    layer, flags_ref, received_ref, z_ref, u_ref, wout_ref, win_ref, unew_ref, znew_ref, send_ref, *refs
):
    *more, high_ref, low_ref, high2_ref, low2_ref, ending_ref, begun_ref = refs
    held, onto = (high_ref, low_ref), (high2_ref, low2_ref)
    split_weights(wout_ref, layer, ending_ref)
    normalise(received_ref, flags_ref[0], z_ref, held)
    if layer == 0:
        rest_ref, packed_ref = more
        packed_ref[0] = win_ref[0]
        packed_ref[1] = wout_ref[0]
        clear_edges(*onto)
        for row, block in branch_blocks(held, ending_ref):
            before = u_ref[row]
            after = before + STEP_SIZE * block
            unew_ref[row] = after
            place(row, after, *onto)
            coarse = before + FACTOR * STEP_SIZE * block
            rest_ref[row] = coarse - (before + FACTOR * (after - before))
    else:
        add_branch(held, ending_ref, STEP_SIZE, u_ref, unew_ref, onto)
    split_weights(win_ref, layer + 1, begun_ref)
    into_conv(onto, begun_ref, znew_ref, send_ref)


def turn_kernel(
    flags_ref, received_ref, z_ref, u_ref, wout_ref, moved_ref, both_ref, ends_ref, send_ref, high_ref, low_ref, high2_ref, low2_ref, ending_ref, weights_ref
):
    held, onto = (high_ref, low_ref), (high2_ref, low2_ref)
    clear_edges(*onto)
    split_weights(wout_ref, FACTOR - 1, ending_ref)
    normalise(received_ref, flags_ref[0], z_ref, held)
    for row, block in branch_blocks(held, ending_ref):
        after = u_ref[row] + STEP_SIZE * block
        both_ref[0, row] = after
        ends_ref[row] = after
        place(row, after, *onto)

    @pl.when(flags_ref[1] == 1)
    def _():
        split_weights(moved_ref, 0, weights_ref)
        into_conv(onto, weights_ref, both_ref.at[1], send_ref)


def fork_kernel(
    flags_ref, received_ref, arrived_ref, both_ref, rest_ref, wout_ref, win_ref, moved_ref,
    unew_ref, znew_ref, send_ref, high_ref, low_ref, high2_ref, low2_ref, ending_ref, weights_ref,
):
    held, onto = (high_ref, low_ref), (high2_ref, low2_ref)

    @pl.when(flags_ref[1] == 1)
    def _():
        clear_edges(*held)
        for row in range(ROWS):
            value = both_ref[0, row] + rest_ref[row]
            unew_ref[row] = value
            place(row, value, *held)
        split_weights(moved_ref, 0, weights_ref)
        into_conv(held, weights_ref, znew_ref, send_ref)

    @pl.when(flags_ref[1] == 0)
    def _():
        split_weights(wout_ref, 0, ending_ref)
        normalise(received_ref, 0, arrived_ref.at[1], held)
        add_branch(held, ending_ref, STEP_SIZE, arrived_ref.at[0], unew_ref, onto)
        split_weights(win_ref, 1, weights_ref)
        into_conv(onto, weights_ref, znew_ref, send_ref)


def coarse_kernel(
    flags_ref, received_ref, z_ref, u_ref, wout_ref, win_ref, moved_ref,
    unew_ref, znew_ref, send_ref, high_ref, low_ref, high2_ref, low2_ref, ending_ref, weights_ref,
):
    held, onto = (high_ref, low_ref), (high2_ref, low2_ref)
    normalise(received_ref, flags_ref[0], z_ref, held)

    @pl.when(flags_ref[1] == 1)
    def _():
        split_weights(moved_ref, 1, weights_ref)
        add_branch(held, weights_ref, FACTOR * STEP_SIZE, u_ref, unew_ref)

    @pl.when(flags_ref[1] == 0)
    def _():
        split_weights(wout_ref, 1, ending_ref)
        add_branch(held, ending_ref, STEP_SIZE, u_ref, unew_ref, onto)
        split_weights(win_ref, 2, weights_ref)
        into_conv(onto, weights_ref, znew_ref, send_ref)


def second_kernel(flags_ref, *refs):
    @pl.when(flags_ref[1] == 0)
    def _():
        step_kernel(2, flags_ref, *refs)


def close_kernel(
    flags_ref, received_ref, z_ref, u_ref, wout_ref, arrived_ref, first_ref, coarse_ref, out_ref, *held
):
    @pl.when(flags_ref[1] == 1)
    def _():
        out_ref[...] = first_ref[...]

    @pl.when(flags_ref[1] == 0)
    def _():
        *states, weights_ref = held
        split_weights(wout_ref, FACTOR - 1, weights_ref)
        normalise(received_ref, flags_ref[0], z_ref, states)
        for row, block in branch_blocks(states, weights_ref):
            fine = u_ref[row] + STEP_SIZE * block
            begun, first = arrived_ref[0, row], first_ref[row]
            tau = fine - (begun + FACTOR * (first - begun))
            out_ref[row] = coarse_ref[row] + tau


STATE = jax.ShapeDtypeStruct((ROWS, COLS, CHANNELS), jnp.float32)
BOTH = jax.ShapeDtypeStruct((2, ROWS, COLS, CHANNELS), jnp.float32)
SMEM = pl.BlockSpec(memory_space=pltpu.SMEM)
VMEM = pl.BlockSpec(memory_space=pltpu.VMEM)
HELD = [pltpu.VMEM(((PAIRS + 1) * COLS, 2 * CHANNELS), jnp.bfloat16)] * 2
WEIGHTS = [pltpu.VMEM((2, 3, 3, CHANNELS, CHANNELS), jnp.bfloat16)]
ONE = HELD + WEIGHTS
TWO = HELD * 2 + WEIGHTS * 2
CONV_FLOPS = 2 * 3 * 512 * 1536 * 256


def call(kernel, name, outs, convs, scratch, *args):
    touched = sum(a.size * a.dtype.itemsize for a in (*args, *outs))
    return pl.pallas_call(
        kernel,
        name=name,
        out_shape=tuple(outs),
        in_specs=[SMEM] + [VMEM] * (len(args) - 1),
        out_specs=(VMEM,) * len(outs),
        scratch_shapes=scratch,
        compiler_params=pltpu.CompilerParams(vmem_limit_bytes=VMEM_LIMIT),
        cost_estimate=pl.CostEstimate(
            flops=convs * CONV_FLOPS, bytes_accessed=touched, transcendentals=0
        ),
    )(*args)


def ready(flags, initial, conv_in):
    shape = conv_in.shape[1:]
    return pl.pallas_call(
        ready_kernel,
        name="ready",
        out_shape=(STATE, jax.ShapeDtypeStruct((2,) + shape, jnp.bfloat16)),
        in_specs=[SMEM] + [pl.BlockSpec(memory_space=pltpu.HBM)] * 2,
        out_specs=(VMEM,) * 2,
        scratch_shapes=[
            pltpu.VMEM((1,) + shape, jnp.float32),
            pltpu.SemaphoreType.DMA((2,)),
        ],
        compiler_params=pltpu.CompilerParams(vmem_limit_bytes=READY_LIMIT),
        cost_estimate=pl.CostEstimate(flops=1000, bytes_accessed=3000000, transcendentals=0),
    )(flags, *(pltpu.with_memory_space_constraint(x, pltpu.HBM) for x in (initial, conv_in)))


def swapped(x):
    return lax.ppermute(x, "depth", [(0, 1), (1, 0)])


def exchange(send):
    return lax.all_to_all(send, WORLD, 0, 0)


def body(initial, guess, conv_in, conv_out):
    devices = lax.axis_size(WORLD)
    sent = jax.ShapeDtypeStruct((devices, 2, CHANNELS), jnp.float32)
    position = lax.axis_index("depth")
    flags = jnp.stack([position * (devices // 2), 1 - position]).astype(jnp.int32)
    outs = (STATE, STATE, sent)

    before = swapped(guess[0, 0])
    held, weights = ready(flags, initial[0], conv_in)
    z, u, send = call(open_kernel, "open", outs, 1, HELD, flags, held, before, weights)
    received = exchange(send)
    packed = jax.ShapeDtypeStruct((2,) + conv_in.shape[1:], jnp.float32)
    u, z, send, rest, packed = call(
        functools.partial(step_kernel, 0), "step", outs + (STATE, packed), 2, TWO,
        flags, received, z, u, conv_out, conv_in,
    )
    moved = swapped(packed)
    received = exchange(send)
    for layer in (1, 2):
        u, z, send = call(
            functools.partial(step_kernel, layer), "step", outs, 2, TWO,
            flags, received, z, u, conv_out, conv_in,
        )
        received = exchange(send)
    both, ends, send = call(
        turn_kernel, "turn", (BOTH, STATE, sent), 2, TWO,
        flags, received, z, u, conv_out, moved,
    )
    arrived = swapped(both)
    received = exchange(send)
    first, z, send = call(
        fork_kernel, "fork", outs, 2, TWO,
        flags, received, arrived, both, rest, conv_out, conv_in, moved,
    )
    received = exchange(send)
    u, z, send = call(
        coarse_kernel, "coarse", outs, 2, TWO,
        flags, received, z, first, conv_out, conv_in, moved,
    )
    coarse = swapped(u)
    received = exchange(send)
    u, z, send = call(
        second_kernel, "second", outs, 2, TWO, flags, received, z, u, conv_out, conv_in
    )
    received = exchange(send)
    (result,) = call(
        close_kernel, "close", (STATE,), 1, ONE,
        flags, received, z, u, conv_out, arrived, first, coarse,
    )
    return (result[None, None], ends[None, None])


def solution(mesh):
    split_mesh = Mesh(
        mesh.devices.reshape(mesh.shape["depth"], 4, 4, 4),
        ("depth", "batch_0", "batch_1", "batch_2"),
    )
    placed = (
        P(BATCH, None, None, None),
        P("depth", BATCH, None, None, None),
        P("depth", None, None, None, None),
        P("depth", None, None, None, None),
    )
    return jax.shard_map(
        body,
        mesh=split_mesh,
        in_specs=placed,
        out_specs=(P("depth", BATCH, None, None, None), P("depth", BATCH, None, None, None)),
        check_vma=False,
    )
```

```python
import functools

import jax
import jax.numpy as jnp
from jax import lax
from jax.experimental import pallas as pl
from jax.experimental.pallas import tpu as pltpu
from jax.sharding import Mesh
from jax.sharding import PartitionSpec as P

FACTOR = 4
BATCH = ("batch_0", "batch_1", "batch_2")
WORLD = ("depth",) + BATCH

EPSILON = 1e-05
STEP_SIZE = 0.25

ROWS = 32
COLS = 32
CHANNELS = 128
PAIRS = ROWS // 2
CELLS = ROWS * COLS
CHUNKS = 2
PART = PAIRS // CHUNKS
VMEM_LIMIT = 24 * 2**20
READY_LIMIT = 24 * 2**20


def split(x):
    high = x.astype(jnp.bfloat16)
    low = (x - high.astype(jnp.float32)).astype(jnp.bfloat16)
    return high, low


def placer(held_ref):
    rows = {-1: jnp.zeros((COLS, CHANNELS), jnp.float32)}

    def put(pair):
        d0, d1, d2, d3 = (rows[2 * pair + i] for i in range(-1, 3))
        del rows[2 * pair - 1], rows[2 * pair]
        at = slice(pair * COLS, (pair + 1) * COLS)
        for kind, value in enumerate((d0 - d2, d1 + d2, d2 - d1, d1 - d3)):
            high, low = split(value)
            held_ref[kind, at, :CHANNELS] = high
            held_ref[kind, at, CHANNELS:] = low

    def add(row, value):
        rows[row] = value
        if row and row % 2 == 0:
            put(row // 2 - 1)
        if row == ROWS - 1:
            rows[ROWS] = rows_end
            put(PAIRS - 1)

    rows_end = rows[-1]
    return add


def convolve(held_ref, weights_ref, chunk):
    many = PART * COLS
    at = slice(chunk * many, (chunk + 1) * many)
    wide = 3 * CHANNELS

    def product(kind):
        right = weights_ref[kind]
        out = jnp.dot(
            held_ref[kind, at, :],
            jnp.concatenate([right, right], axis=0),
            preferred_element_type=jnp.float32,
        )
        return out[:, :wide] + out[:, wide:]

    m0, m1, m2, m3 = (product(kind) for kind in range(4))
    column = lax.broadcasted_iota(jnp.int32, (many, CHANNELS), 0) % COLS

    def across(x):
        left, middle, right = (x[:, i * CHANNELS : (i + 1) * CHANNELS] for i in range(3))
        out = middle + jnp.where(column == 0, 0.0, pltpu.roll(left, 1, 0))
        return out + jnp.where(column == COLS - 1, 0.0, pltpu.roll(right, many - 1, 0))

    return across(m0 + (m1 + m2)), across((m1 - m2) - m3)


def branch_blocks(held_ref, weights_ref):
    for chunk in range(CHUNKS):
        halves = convolve(held_ref, weights_ref, chunk)
        for pair in range(PART):
            for half in range(2):
                yield 2 * (chunk * PART + pair) + half, halves[half][pair * COLS : (pair + 1) * COLS]


def into_conv(held_ref, weights_ref, z_ref, send_ref):
    totals, squares = [], []
    for chunk in range(CHUNKS):
        halves = convolve(held_ref, weights_ref, chunk)
        for half, out in enumerate(halves):
            for pair in range(PART):
                z_ref[2 * (chunk * PART + pair) + half] = out[pair * COLS : (pair + 1) * COLS]
            total = jnp.sum(out, axis=0, keepdims=True)
            away = out - total * (1.0 / (PART * COLS))
            totals.append(total)
            squares.append(jnp.sum(away * away, axis=0, keepdims=True))
    total = functools.reduce(jnp.add, totals)
    square = functools.reduce(jnp.add, squares)
    for part in totals:
        away = part * (1.0 / (PART * COLS)) - total * (1.0 / CELLS)
        square = square + (PART * COLS) * (away * away)
    both = jnp.concatenate([total, square], axis=0)
    send_ref[...] = jnp.broadcast_to(both[None], send_ref.shape)


def combined(received_ref, base):
    rows = received_ref[pl.ds(base, received_ref.shape[0] // 2)]
    samples = rows.shape[0]
    totals = rows[:, 0:1, :]
    average = jnp.sum(totals, axis=0) * (1.0 / (samples * CELLS))
    away = totals * (1.0 / CELLS) - average[None]
    square = jnp.sum(rows[:, 1:2, :], axis=0) + CELLS * jnp.sum(away * away, axis=0)
    return average, lax.rsqrt(square * (1.0 / (samples * CELLS)) + EPSILON)


def normalise(received_ref, base, z_ref, held_ref):
    average, factor = combined(received_ref, base)
    put = placer(held_ref)
    for row in range(ROWS):
        put(row, jnp.maximum((z_ref[row] - average) * factor, 0.0))


def add_branch(held_ref, weights_ref, scale, u_ref, unew_ref, onto_ref=None):
    put = placer(onto_ref) if onto_ref is not None else None
    for row, block in branch_blocks(held_ref, weights_ref):
        after = u_ref[row] + scale * block
        unew_ref[row] = after
        if put:
            put(row, after)


def split_weights(raw_ref, at, weights_ref):
    for across in range(3):
        first, middle, last = (raw_ref[at, up, across] for up in range(3))
        outer, inner = 0.5 * (first + last), 0.5 * middle
        for kind, value in enumerate((first, outer + inner, outer - inner, last)):
            high, low = split(value)
            weights_ref[kind, :, across * CHANNELS : (across + 1) * CHANNELS] = high
            weights_ref[kind, :, (3 + across) * CHANNELS : (4 + across) * CHANNELS] = low


def ready_kernel(flags_ref, initial_hbm, win_hbm, initial_ref, weights_ref, raw_ref, sem):
    weights = pltpu.make_async_copy(win_hbm.at[pl.ds(0, 1)], raw_ref, sem.at[0])
    state = pltpu.make_async_copy(initial_hbm, initial_ref, sem.at[1])
    weights.start()
    state.start()
    weights.wait()
    split_weights(raw_ref, 0, weights_ref)
    state.wait()


def open_kernel(flags_ref, initial_ref, before_ref, weights_ref, z_ref, u_ref, send_ref, held_ref):
    first = flags_ref[1] == 1
    put = placer(held_ref)
    for row in range(ROWS):
        value = jnp.where(first, initial_ref[row], before_ref[row])
        u_ref[row] = value
        put(row, value)
    into_conv(held_ref, weights_ref, z_ref, send_ref)


def step_kernel(
    layer, flags_ref, received_ref, z_ref, u_ref, wout_ref, win_ref, unew_ref, znew_ref, send_ref, *refs
):
    *more, held_ref, onto_ref, ending_ref, begun_ref = refs
    split_weights(wout_ref, layer, ending_ref)
    normalise(received_ref, flags_ref[0], z_ref, held_ref)
    if layer == 0:
        rest_ref, packed_ref = more
        packed_ref[0] = win_ref[0]
        packed_ref[1] = wout_ref[0]
        put = placer(onto_ref)
        for row, block in branch_blocks(held_ref, ending_ref):
            before = u_ref[row]
            after = before + STEP_SIZE * block
            unew_ref[row] = after
            put(row, after)
            coarse = before + FACTOR * STEP_SIZE * block
            rest_ref[row] = coarse - (before + FACTOR * (after - before))
    else:
        add_branch(held_ref, ending_ref, STEP_SIZE, u_ref, unew_ref, onto_ref)
    split_weights(win_ref, layer + 1, begun_ref)
    into_conv(onto_ref, begun_ref, znew_ref, send_ref)


def turn_kernel(
    flags_ref, received_ref, z_ref, u_ref, wout_ref, moved_ref, both_ref, ends_ref, send_ref,
    held_ref, onto_ref, ending_ref, begun_ref,
):
    split_weights(wout_ref, FACTOR - 1, ending_ref)
    normalise(received_ref, flags_ref[0], z_ref, held_ref)
    put = placer(onto_ref)
    for row, block in branch_blocks(held_ref, ending_ref):
        after = u_ref[row] + STEP_SIZE * block
        both_ref[0, row] = after
        ends_ref[row] = after
        put(row, after)
    split_weights(moved_ref, 0, begun_ref)
    into_conv(onto_ref, begun_ref, both_ref.at[1], send_ref)


def fork_kernel(
    flags_ref, received_ref, arrived_ref, both_ref, rest_ref, wout_ref, win_ref, moved_ref,
    unew_ref, znew_ref, send_ref, held_ref, onto_ref, ending_ref, begun_ref,
):
    @pl.when(flags_ref[1] == 1)
    def _():
        put = placer(held_ref)
        for row in range(ROWS):
            value = both_ref[0, row] + rest_ref[row]
            unew_ref[row] = value
            put(row, value)
        split_weights(moved_ref, 0, begun_ref)
        into_conv(held_ref, begun_ref, znew_ref, send_ref)

    @pl.when(flags_ref[1] == 0)
    def _():
        split_weights(wout_ref, 0, ending_ref)
        normalise(received_ref, 0, arrived_ref.at[1], held_ref)
        add_branch(held_ref, ending_ref, STEP_SIZE, arrived_ref.at[0], unew_ref, onto_ref)
        split_weights(win_ref, 1, begun_ref)
        into_conv(onto_ref, begun_ref, znew_ref, send_ref)


def coarse_kernel(
    flags_ref, received_ref, z_ref, u_ref, wout_ref, win_ref, moved_ref,
    unew_ref, znew_ref, send_ref, held_ref, onto_ref, ending_ref, begun_ref,
):
    @pl.when(flags_ref[1] == 1)
    def _():
        split_weights(moved_ref, 1, ending_ref)
        normalise(received_ref, flags_ref[0], z_ref, held_ref)
        add_branch(held_ref, ending_ref, FACTOR * STEP_SIZE, u_ref, unew_ref)

    @pl.when(flags_ref[1] == 0)
    def _():
        split_weights(wout_ref, 1, ending_ref)
        normalise(received_ref, flags_ref[0], z_ref, held_ref)
        add_branch(held_ref, ending_ref, STEP_SIZE, u_ref, unew_ref, onto_ref)
        split_weights(win_ref, 2, begun_ref)
        into_conv(onto_ref, begun_ref, znew_ref, send_ref)


def second_kernel(flags_ref, *refs):
    @pl.when(flags_ref[1] == 0)
    def _():
        step_kernel(2, flags_ref, *refs)


def close_kernel(
    flags_ref, received_ref, z_ref, u_ref, wout_ref, arrived_ref, first_ref, coarse_ref, out_hbm,
    held_ref, ending_ref, out_ref, sem,
):
    @pl.when(flags_ref[1] == 1)
    def _():
        copy = pltpu.make_async_copy(first_ref, out_hbm, sem.at[0])
        copy.start()
        copy.wait()

    @pl.when(flags_ref[1] == 0)
    def _():
        split_weights(wout_ref, FACTOR - 1, ending_ref)
        normalise(received_ref, flags_ref[0], z_ref, held_ref)
        copies = []
        for row, block in branch_blocks(held_ref, ending_ref):
            fine = u_ref[row] + STEP_SIZE * block
            begun, first = arrived_ref[0, row], first_ref[row]
            tau = fine - (begun + FACTOR * (first - begun))
            out_ref[row] = coarse_ref[row] + tau
            if (row + 1) % (2 * PART) == 0:
                rows = pl.ds(row + 1 - 2 * PART, 2 * PART)
                copies.append(
                    pltpu.make_async_copy(out_ref.at[rows], out_hbm.at[rows], sem.at[len(copies)])
                )
                copies[-1].start()
        for copy in copies:
            copy.wait()


STATE = jax.ShapeDtypeStruct((ROWS, COLS, CHANNELS), jnp.float32)
BOTH = jax.ShapeDtypeStruct((2, ROWS, COLS, CHANNELS), jnp.float32)
SMEM = pl.BlockSpec(memory_space=pltpu.SMEM)
VMEM = pl.BlockSpec(memory_space=pltpu.VMEM)
HELD = [pltpu.VMEM((4, PAIRS * COLS, 2 * CHANNELS), jnp.bfloat16)]
WEIGHTS = [pltpu.VMEM((4, CHANNELS, 6 * CHANNELS), jnp.bfloat16)]
ONE = HELD + WEIGHTS
TWO = HELD * 2 + WEIGHTS * 2
CLOSE = ONE + [
    pltpu.VMEM((ROWS, COLS, CHANNELS), jnp.float32),
    pltpu.SemaphoreType.DMA((CHUNKS,)),
]
CONV_FLOPS = 2 * 4 * 512 * 256 * 768


def call(kernel, name, outs, convs, scratch, *args, out_space=VMEM):
    touched = sum(a.size * a.dtype.itemsize for a in (*args, *outs))
    return pl.pallas_call(
        kernel,
        name=name,
        out_shape=tuple(outs),
        in_specs=[SMEM] + [VMEM] * (len(args) - 1),
        out_specs=(out_space,) * len(outs),
        scratch_shapes=scratch,
        compiler_params=pltpu.CompilerParams(vmem_limit_bytes=VMEM_LIMIT),
        cost_estimate=pl.CostEstimate(
            flops=convs * CONV_FLOPS, bytes_accessed=touched, transcendentals=0
        ),
    )(*args)


def ready(flags, initial, conv_in):
    shape = conv_in.shape[1:]
    return pl.pallas_call(
        ready_kernel,
        name="ready",
        out_shape=(STATE, jax.ShapeDtypeStruct(WEIGHTS[0].shape, jnp.bfloat16)),
        in_specs=[SMEM] + [pl.BlockSpec(memory_space=pltpu.HBM)] * 2,
        out_specs=(VMEM,) * 2,
        scratch_shapes=[
            pltpu.VMEM((1,) + shape, jnp.float32),
            pltpu.SemaphoreType.DMA((2,)),
        ],
        compiler_params=pltpu.CompilerParams(vmem_limit_bytes=READY_LIMIT),
        cost_estimate=pl.CostEstimate(flops=1000, bytes_accessed=3000000, transcendentals=0),
    )(flags, *(pltpu.with_memory_space_constraint(x, pltpu.HBM) for x in (initial, conv_in)))


def swapped(x):
    return lax.ppermute(x, "depth", [(0, 1), (1, 0)])


def exchange(send):
    return lax.all_to_all(send, WORLD, 0, 0)


def body(initial, guess, conv_in, conv_out):
    devices = lax.axis_size(WORLD)
    sent = jax.ShapeDtypeStruct((devices, 2, CHANNELS), jnp.float32)
    position = lax.axis_index("depth")
    flags = jnp.stack([position * (devices // 2), 1 - position]).astype(jnp.int32)
    outs = (STATE, STATE, sent)

    before = swapped(guess[0, 0])
    held, weights = ready(flags, initial[0], conv_in)
    z, u, send = call(open_kernel, "open", outs, 1, HELD, flags, held, before, weights)
    received = exchange(send)
    packed = jax.ShapeDtypeStruct((2,) + conv_in.shape[1:], jnp.float32)
    u, z, send, rest, packed = call(
        functools.partial(step_kernel, 0), "step", outs + (STATE, packed), 2, TWO,
        flags, received, z, u, conv_out, conv_in,
    )
    moved = swapped(packed)
    received = exchange(send)
    for layer in (1, 2):
        u, z, send = call(
            functools.partial(step_kernel, layer), "step", outs, 2, TWO,
            flags, received, z, u, conv_out, conv_in,
        )
        received = exchange(send)
    both, ends, send = call(
        turn_kernel, "turn", (BOTH, STATE, sent), 2, TWO,
        flags, received, z, u, conv_out, moved,
    )
    arrived = swapped(both)
    received = exchange(send)
    first, z, send = call(
        fork_kernel, "fork", outs, 2, TWO,
        flags, received, arrived, both, rest, conv_out, conv_in, moved,
    )
    received = exchange(send)
    u, z, send = call(
        coarse_kernel, "coarse", outs, 2, TWO,
        flags, received, z, first, conv_out, conv_in, moved,
    )
    coarse = swapped(u)
    received = exchange(send)
    u, z, send = call(
        second_kernel, "second", outs, 2, TWO, flags, received, z, u, conv_out, conv_in
    )
    received = exchange(send)
    (result,) = call(
        close_kernel, "close", (STATE,), 1, CLOSE,
        flags, received, z, u, conv_out, arrived, first, coarse, out_space=pl.BlockSpec(memory_space=pltpu.HBM),
    )
    return (result[None, None], ends[None, None])


def solution(mesh):
    split_mesh = Mesh(
        mesh.devices.reshape(mesh.shape["depth"], 4, 4, 4),
        ("depth", "batch_0", "batch_1", "batch_2"),
    )
    placed = (
        P(BATCH, None, None, None),
        P("depth", BATCH, None, None, None),
        P("depth", None, None, None, None),
        P("depth", None, None, None, None),
    )
    return jax.shard_map(
        body,
        mesh=split_mesh,
        in_specs=placed,
        out_specs=(P("depth", BATCH, None, None, None), P("depth", BATCH, None, None, None)),
        check_vma=False,
    )
```

```python
import functools

import jax
import jax.numpy as jnp
from jax import lax
from jax.experimental import pallas as pl
from jax.experimental.pallas import tpu as pltpu
from jax.sharding import Mesh
from jax.sharding import PartitionSpec as P

FACTOR = 4
BATCH = ("batch_0", "batch_1", "batch_2")
WORLD = ("depth",) + BATCH

EPSILON = 1e-05
STEP_SIZE = 0.25

ROWS = 32
COLS = 32
CHANNELS = 128
PAIRS = ROWS // 2
CELLS = ROWS * COLS
CHUNKS = 2
PART = PAIRS // CHUNKS
VMEM_LIMIT = 24 * 2**20
READY_LIMIT = 24 * 2**20


def split(x):
    high = x.astype(jnp.bfloat16)
    low = (x - high.astype(jnp.float32)).astype(jnp.bfloat16)
    return high, low


def placer(held_ref):
    rows = {-1: jnp.zeros((COLS, CHANNELS), jnp.float32)}

    def put(pair):
        d0, d1, d2, d3 = (rows[2 * pair + i] for i in range(-1, 3))
        del rows[2 * pair - 1], rows[2 * pair]
        at = slice(pair * COLS, (pair + 1) * COLS)
        for kind, value in enumerate((d0 - d2, d1 + d2, d2 - d1, d1 - d3)):
            high, low = split(value)
            held_ref[kind, at, :CHANNELS] = high
            held_ref[kind, at, CHANNELS:] = low

    def add(row, value):
        rows[row] = value
        if row and row % 2 == 0:
            put(row // 2 - 1)
        if row == ROWS - 1:
            rows[ROWS] = rows_end
            put(PAIRS - 1)

    rows_end = rows[-1]
    return add


def convolve(held_ref, weights_ref, chunk):
    many = PART * COLS
    at = slice(chunk * many, (chunk + 1) * many)
    wide = 3 * CHANNELS

    def product(kind):
        right = weights_ref[kind]
        out = jnp.dot(
            held_ref[kind, at, :],
            jnp.concatenate([right, right], axis=0),
            preferred_element_type=jnp.float32,
        )
        return out[:, :wide] + out[:, wide:]

    m0, m1, m2, m3 = (product(kind) for kind in range(4))
    column = lax.broadcasted_iota(jnp.int32, (many, CHANNELS), 0) % COLS

    def across(x):
        left, middle, right = (x[:, i * CHANNELS : (i + 1) * CHANNELS] for i in range(3))
        out = middle + jnp.where(column == 0, 0.0, pltpu.roll(left, 1, 0))
        return out + jnp.where(column == COLS - 1, 0.0, pltpu.roll(right, many - 1, 0))

    return across(m0 + (m1 + m2)), across((m1 - m2) - m3)


def branch_blocks(held_ref, weights_ref):
    for chunk in range(CHUNKS):
        halves = convolve(held_ref, weights_ref, chunk)
        for pair in range(PART):
            for half in range(2):
                yield 2 * (chunk * PART + pair) + half, halves[half][pair * COLS : (pair + 1) * COLS]


def into_conv(held_ref, weights_ref, z_ref, send_ref):
    totals, squares = [], []
    for chunk in range(CHUNKS):
        halves = convolve(held_ref, weights_ref, chunk)
        for half, out in enumerate(halves):
            for pair in range(PART):
                z_ref[2 * (chunk * PART + pair) + half] = out[pair * COLS : (pair + 1) * COLS]
            total = jnp.sum(out, axis=0, keepdims=True)
            away = out - total * (1.0 / (PART * COLS))
            totals.append(total)
            squares.append(jnp.sum(away * away, axis=0, keepdims=True))
    total = functools.reduce(jnp.add, totals)
    square = functools.reduce(jnp.add, squares)
    for part in totals:
        away = part * (1.0 / (PART * COLS)) - total * (1.0 / CELLS)
        square = square + (PART * COLS) * (away * away)
    is_sum = lax.broadcasted_iota(jnp.int32, send_ref.shape, 0) % 2 == 0
    send_ref[...] = jnp.where(is_sum, total, square)


def combined(received_ref, base):
    samples = received_ref.shape[0] // 4
    rows = received_ref[pl.ds(pl.multiple_of(2 * base, 2 * samples), 2 * samples), :]
    is_sum = lax.broadcasted_iota(jnp.int32, rows.shape, 0) % 2 == 0
    average = jnp.sum(jnp.where(is_sum, rows, 0.0), axis=0, keepdims=True) * (1.0 / (samples * CELLS))
    away = rows * (1.0 / CELLS) - average
    square = jnp.sum(jnp.where(is_sum, CELLS * (away * away), rows), axis=0, keepdims=True)
    return average, lax.rsqrt(square * (1.0 / (samples * CELLS)) + EPSILON)


def normalise(received_ref, base, z_ref, held_ref):
    average, factor = combined(received_ref, base)
    put = placer(held_ref)
    for row in range(ROWS):
        put(row, jnp.maximum((z_ref[row] - average) * factor, 0.0))


def add_branch(held_ref, weights_ref, scale, u_ref, unew_ref, onto_ref=None):
    put = placer(onto_ref) if onto_ref is not None else None
    for row, block in branch_blocks(held_ref, weights_ref):
        after = u_ref[row] + scale * block
        unew_ref[row] = after
        if put:
            put(row, after)


def split_weights(raw_ref, at, weights_ref):
    for across in range(3):
        first, middle, last = (raw_ref[at, up, across] for up in range(3))
        outer, inner = 0.5 * (first + last), 0.5 * middle
        for kind, value in enumerate((first, outer + inner, outer - inner, last)):
            high, low = split(value)
            weights_ref[kind, :, across * CHANNELS : (across + 1) * CHANNELS] = high
            weights_ref[kind, :, (3 + across) * CHANNELS : (4 + across) * CHANNELS] = low


def ready_kernel(flags_ref, initial_hbm, win_hbm, initial_ref, weights_ref, raw_ref, sem):
    weights = pltpu.make_async_copy(win_hbm.at[pl.ds(0, 1)], raw_ref, sem.at[0])
    state = pltpu.make_async_copy(initial_hbm, initial_ref, sem.at[1])
    weights.start()
    state.start()
    weights.wait()
    split_weights(raw_ref, 0, weights_ref)
    state.wait()


def open_kernel(flags_ref, initial_ref, before_ref, weights_ref, z_ref, u_ref, send_ref, held_ref):
    first = flags_ref[1] == 1
    put = placer(held_ref)
    for row in range(ROWS):
        value = jnp.where(first, initial_ref[row], before_ref[row])
        u_ref[row] = value
        put(row, value)
    into_conv(held_ref, weights_ref, z_ref, send_ref)


def fine_step(flags_ref, received_ref, z_ref, u_ref, ending_ref, begun_ref, unew_ref, znew_ref, send_ref, held_ref, onto_ref):
    normalise(received_ref, flags_ref[0], z_ref, held_ref)
    add_branch(held_ref, ending_ref, STEP_SIZE, u_ref, unew_ref, onto_ref)
    into_conv(onto_ref, begun_ref, znew_ref, send_ref)


def begin_kernel(
    flags_ref, received_ref, z_ref, u_ref, wout_ref, win_ref,
    unew_ref, znew_ref, send_ref, ending_ref, begun_ref, rest_ref, packed_ref, held_ref, onto_ref,
):
    split_weights(wout_ref, 0, ending_ref)
    normalise(received_ref, flags_ref[0], z_ref, held_ref)
    put = placer(onto_ref)
    for row, block in branch_blocks(held_ref, ending_ref):
        before = u_ref[row]
        after = before + STEP_SIZE * block
        unew_ref[row] = after
        put(row, after)
        coarse = before + FACTOR * STEP_SIZE * block
        rest_ref[row] = coarse - (before + FACTOR * (after - before))
    packed_ref[0] = win_ref[0]
    packed_ref[1] = wout_ref[0]
    split_weights(win_ref, 1, begun_ref)
    into_conv(onto_ref, begun_ref, znew_ref, send_ref)


def step_kernel(
    layer, flags_ref, received_ref, z_ref, u_ref, wout_ref, win_ref,
    unew_ref, znew_ref, send_ref, ending_ref, begun_ref, held_ref, onto_ref,
):
    split_weights(wout_ref, layer, ending_ref)
    normalise(received_ref, flags_ref[0], z_ref, held_ref)
    add_branch(held_ref, ending_ref, STEP_SIZE, u_ref, unew_ref, onto_ref)
    split_weights(win_ref, layer + 1, begun_ref)
    into_conv(onto_ref, begun_ref, znew_ref, send_ref)


def turn_kernel(
    flags_ref, received_ref, z_ref, u_ref, wout_ref, moved_ref,
    both_ref, ends_ref, send_ref, ending_ref, begun_ref, held_ref, onto_ref,
):
    split_weights(wout_ref, FACTOR - 1, ending_ref)
    normalise(received_ref, flags_ref[0], z_ref, held_ref)
    put = placer(onto_ref)
    for row, block in branch_blocks(held_ref, ending_ref):
        after = u_ref[row] + STEP_SIZE * block
        both_ref[0, row] = after
        ends_ref[row] = after
        put(row, after)
    split_weights(moved_ref, 0, begun_ref)
    into_conv(onto_ref, begun_ref, both_ref.at[1], send_ref)


def fork_kernel(
    flags_ref, received_ref, arrived_ref, both_ref, rest_ref, moved_ref, ending_ref, begun_ref,
    unew_ref, znew_ref, send_ref, held_ref, onto_ref,
):
    @pl.when(flags_ref[1] == 1)
    def _():
        put = placer(held_ref)
        for row in range(ROWS):
            value = both_ref[0, row] + rest_ref[row]
            unew_ref[row] = value
            put(row, value)
        into_conv(held_ref, moved_ref, znew_ref, send_ref)

    @pl.when(flags_ref[1] == 0)
    def _():
        normalise(received_ref, 0, arrived_ref.at[1], held_ref)
        add_branch(held_ref, ending_ref, STEP_SIZE, arrived_ref.at[0], unew_ref, onto_ref)
        into_conv(onto_ref, begun_ref, znew_ref, send_ref)


def coarse_kernel(
    flags_ref, received_ref, z_ref, u_ref, moved_ref, ending_ref, begun_ref,
    unew_ref, znew_ref, send_ref, held_ref, onto_ref, weights_ref,
):
    @pl.when(flags_ref[1] == 1)
    def _():
        split_weights(moved_ref, 1, weights_ref)
        normalise(received_ref, flags_ref[0], z_ref, held_ref)
        add_branch(held_ref, weights_ref, FACTOR * STEP_SIZE, u_ref, unew_ref)

    @pl.when(flags_ref[1] == 0)
    def _():
        fine_step(
            flags_ref, received_ref, z_ref, u_ref, ending_ref, begun_ref,
            unew_ref, znew_ref, send_ref, held_ref, onto_ref,
        )


def second_kernel(flags_ref, *refs):
    @pl.when(flags_ref[1] == 0)
    def _():
        fine_step(flags_ref, *refs)


def close_kernel(
    flags_ref, received_ref, z_ref, u_ref, ending_ref, arrived_ref, first_ref, coarse_ref, out_hbm,
    held_ref, out_ref, sem,
):
    @pl.when(flags_ref[1] == 1)
    def _():
        copy = pltpu.make_async_copy(first_ref, out_hbm, sem.at[0])
        copy.start()
        copy.wait()

    @pl.when(flags_ref[1] == 0)
    def _():
        normalise(received_ref, flags_ref[0], z_ref, held_ref)
        copies = []
        for row, block in branch_blocks(held_ref, ending_ref):
            fine = u_ref[row] + STEP_SIZE * block
            begun, first = arrived_ref[0, row], first_ref[row]
            tau = fine - (begun + FACTOR * (first - begun))
            out_ref[row] = coarse_ref[row] + tau
            if (row + 1) % (2 * PART) == 0:
                rows = pl.ds(row + 1 - 2 * PART, 2 * PART)
                copies.append(
                    pltpu.make_async_copy(out_ref.at[rows], out_hbm.at[rows], sem.at[len(copies)])
                )
                copies[-1].start()
        for copy in copies:
            copy.wait()


STATE = jax.ShapeDtypeStruct((ROWS, COLS, CHANNELS), jnp.float32)
BOTH = jax.ShapeDtypeStruct((2, ROWS, COLS, CHANNELS), jnp.float32)
SMEM = pl.BlockSpec(memory_space=pltpu.SMEM)
VMEM = pl.BlockSpec(memory_space=pltpu.VMEM)
HELD = [pltpu.VMEM((4, PAIRS * COLS, 2 * CHANNELS), jnp.bfloat16)]
WEIGHTS = [pltpu.VMEM((4, CHANNELS, 6 * CHANNELS), jnp.bfloat16)]
READY = jax.ShapeDtypeStruct(WEIGHTS[0].shape, jnp.bfloat16)
TWO = HELD * 2
CLOSE = HELD + [
    pltpu.VMEM((ROWS, COLS, CHANNELS), jnp.float32),
    pltpu.SemaphoreType.DMA((CHUNKS,)),
]
CONV_FLOPS = 2 * 4 * 512 * 256 * 768


def call(kernel, name, outs, convs, scratch, *args, out_space=VMEM):
    touched = sum(a.size * a.dtype.itemsize for a in (*args, *outs))
    return pl.pallas_call(
        kernel,
        name=name,
        out_shape=tuple(outs),
        in_specs=[SMEM] + [VMEM] * (len(args) - 1),
        out_specs=(out_space,) * len(outs),
        scratch_shapes=scratch,
        compiler_params=pltpu.CompilerParams(vmem_limit_bytes=VMEM_LIMIT),
        cost_estimate=pl.CostEstimate(
            flops=convs * CONV_FLOPS, bytes_accessed=touched, transcendentals=0
        ),
    )(*args)


def ready(flags, initial, conv_in):
    shape = conv_in.shape[1:]
    return pl.pallas_call(
        ready_kernel,
        name="ready",
        out_shape=(STATE, READY),
        in_specs=[SMEM] + [pl.BlockSpec(memory_space=pltpu.HBM)] * 2,
        out_specs=(VMEM,) * 2,
        scratch_shapes=[
            pltpu.VMEM((1,) + shape, jnp.float32),
            pltpu.SemaphoreType.DMA((2,)),
        ],
        compiler_params=pltpu.CompilerParams(vmem_limit_bytes=READY_LIMIT),
        cost_estimate=pl.CostEstimate(flops=1000, bytes_accessed=3000000, transcendentals=0),
    )(flags, *(pltpu.with_memory_space_constraint(x, pltpu.HBM) for x in (initial, conv_in)))


def swapped(x):
    return lax.ppermute(x, "depth", [(0, 1), (1, 0)])


def exchange(send):
    apart = send.reshape(send.shape[0] // 2, 2, CHANNELS)
    return lax.all_to_all(apart, WORLD, 0, 0).reshape(send.shape)


def body(initial, guess, conv_in, conv_out):
    devices = lax.axis_size(WORLD)
    sent = jax.ShapeDtypeStruct((2 * devices, CHANNELS), jnp.float32)
    position = lax.axis_index("depth")
    flags = jnp.stack([position * (devices // 2), 1 - position]).astype(jnp.int32)
    outs = (STATE, STATE, sent)

    before = swapped(guess[0, 0])
    held, weights = ready(flags, initial[0], conv_in)
    z, u, send = call(open_kernel, "open", outs, 1, HELD, flags, held, before, weights)
    received = exchange(send)
    packed = jax.ShapeDtypeStruct((2,) + conv_in.shape[1:], jnp.float32)
    u, z, send, ending, begun, rest, packed = call(
        begin_kernel, "begin", outs + (READY, READY, STATE, packed), 2, TWO,
        flags, received, z, u, conv_out, conv_in,
    )
    endings, beginnings = [ending], [None, begun]
    moved = swapped(packed)
    received = exchange(send)
    for layer in (1, 2):
        u, z, send, ending, begun = call(
            functools.partial(step_kernel, layer), "step", outs + (READY, READY), 2, TWO,
            flags, received, z, u, conv_out, conv_in,
        )
        endings.append(ending)
        beginnings.append(begun)
        received = exchange(send)
    both, ends, send, ending, coarse_in = call(
        turn_kernel, "turn", (BOTH, STATE, sent, READY, READY), 2, TWO,
        flags, received, z, u, conv_out, moved,
    )
    endings.append(ending)
    arrived = swapped(both)
    received = exchange(send)
    first, z, send = call(
        fork_kernel, "fork", outs, 2, TWO,
        flags, received, arrived, both, rest, coarse_in, endings[0], beginnings[1],
    )
    received = exchange(send)
    u, z, send = call(
        coarse_kernel, "coarse", outs, 2, TWO + WEIGHTS,
        flags, received, z, first, moved, endings[1], beginnings[2],
    )
    coarse = swapped(u)
    received = exchange(send)
    u, z, send = call(
        second_kernel, "second", outs, 2, TWO, flags, received, z, u, endings[2], beginnings[3]
    )
    received = exchange(send)
    (result,) = call(
        close_kernel, "close", (STATE,), 1, CLOSE,
        flags, received, z, u, endings[3], arrived, first, coarse,
        out_space=pl.BlockSpec(memory_space=pltpu.HBM),
    )
    return (result[None, None], ends[None, None])


def solution(mesh):
    split_mesh = Mesh(
        mesh.devices.reshape(mesh.shape["depth"], 4, 4, 4),
        ("depth", "batch_0", "batch_1", "batch_2"),
    )
    placed = (
        P(BATCH, None, None, None),
        P("depth", BATCH, None, None, None),
        P("depth", None, None, None, None),
        P("depth", None, None, None, None),
    )
    return jax.shard_map(
        body,
        mesh=split_mesh,
        in_specs=placed,
        out_specs=(P("depth", BATCH, None, None, None), P("depth", BATCH, None, None, None)),
        check_vma=False,
    )
```

```python
import functools

import jax
import jax.numpy as jnp
from jax import lax
from jax.experimental import pallas as pl
from jax.experimental.pallas import tpu as pltpu
from jax.sharding import Mesh
from jax.sharding import PartitionSpec as P

FACTOR = 4
BATCH = ("batch_0", "batch_1", "batch_2")
WORLD = ("depth",) + BATCH

EPSILON = 1e-05
STEP_SIZE = 0.25

ROWS = 32
COLS = 32
CHANNELS = 128
PAIRS = ROWS // 2
CELLS = ROWS * COLS
CHUNKS = 2
PART = PAIRS // CHUNKS
VMEM_LIMIT = 24 * 2**20
READY_LIMIT = 24 * 2**20


def split(x):
    high = x.astype(jnp.bfloat16)
    low = (x - high.astype(jnp.float32)).astype(jnp.bfloat16)
    return high, low


def placer(held_ref):
    rows = {-1: jnp.zeros((COLS, CHANNELS), jnp.float32)}

    def put(pair):
        d0, d1, d2, d3 = (rows[2 * pair + i] for i in range(-1, 3))
        del rows[2 * pair - 1], rows[2 * pair]
        at = slice(pair * COLS, (pair + 1) * COLS)
        for kind, value in enumerate((d0 - d2, d1 + d2, d2 - d1, d1 - d3)):
            high, low = split(value)
            held_ref[kind, at, :CHANNELS] = high
            held_ref[kind, at, CHANNELS:] = low

    def add(row, value):
        rows[row] = value
        if row and row % 2 == 0:
            put(row // 2 - 1)
        if row == ROWS - 1:
            rows[ROWS] = rows_end
            put(PAIRS - 1)

    rows_end = rows[-1]
    return add


def convolve(held_ref, weights_ref, chunk):
    many = PART * COLS
    at = slice(chunk * many, (chunk + 1) * many)
    wide = 3 * CHANNELS

    def product(kind):
        right = weights_ref[kind]
        out = jnp.dot(
            held_ref[kind, at, :],
            jnp.concatenate([right, right], axis=0),
            preferred_element_type=jnp.float32,
        )
        return out[:, :wide] + out[:, wide:]

    m0, m1, m2, m3 = (product(kind) for kind in range(4))
    column = lax.broadcasted_iota(jnp.int32, (many, CHANNELS), 0) % COLS

    def across(x):
        left, middle, right = (x[:, i * CHANNELS : (i + 1) * CHANNELS] for i in range(3))
        out = middle + jnp.where(column == 0, 0.0, pltpu.roll(left, 1, 0))
        return out + jnp.where(column == COLS - 1, 0.0, pltpu.roll(right, many - 1, 0))

    return across(m0 + (m1 + m2)), across((m1 - m2) - m3)


def branch_blocks(held_ref, weights_ref):
    for chunk in range(CHUNKS):
        halves = convolve(held_ref, weights_ref, chunk)
        for pair in range(PART):
            for half in range(2):
                yield 2 * (chunk * PART + pair) + half, halves[half][pair * COLS : (pair + 1) * COLS]


def into_conv(held_ref, weights_ref, z_ref, send_ref):
    totals, squares = [], []
    for chunk in range(CHUNKS):
        halves = convolve(held_ref, weights_ref, chunk)
        for half, out in enumerate(halves):
            for pair in range(PART):
                z_ref[2 * (chunk * PART + pair) + half] = out[pair * COLS : (pair + 1) * COLS]
            total = jnp.sum(out, axis=0, keepdims=True)
            away = out - total * (1.0 / (PART * COLS))
            totals.append(total)
            squares.append(jnp.sum(away * away, axis=0, keepdims=True))
    total = functools.reduce(jnp.add, totals)
    square = functools.reduce(jnp.add, squares)
    for part in totals:
        away = part * (1.0 / (PART * COLS)) - total * (1.0 / CELLS)
        square = square + (PART * COLS) * (away * away)
    is_sum = lax.broadcasted_iota(jnp.int32, send_ref.shape, 0) % 2 == 0
    send_ref[...] = jnp.where(is_sum, total, square)


def core():
    return lax.axis_index("depth")


def own_rows(received_ref):
    return core() * (received_ref.shape[0] // 2)


def combined(received_ref, base):
    samples = received_ref.shape[0] // 4
    rows = received_ref[pl.ds(pl.multiple_of(base, 2 * samples), 2 * samples), :]
    is_sum = lax.broadcasted_iota(jnp.int32, rows.shape, 0) % 2 == 0
    average = jnp.sum(jnp.where(is_sum, rows, 0.0), axis=0, keepdims=True) * (1.0 / (samples * CELLS))
    away = rows * (1.0 / CELLS) - average
    square = jnp.sum(jnp.where(is_sum, CELLS * (away * away), rows), axis=0, keepdims=True)
    return average, lax.rsqrt(square * (1.0 / (samples * CELLS)) + EPSILON)


def normalise(received_ref, base, z_ref, held_ref):
    average, factor = combined(received_ref, base)
    put = placer(held_ref)
    for row in range(ROWS):
        put(row, jnp.maximum((z_ref[row] - average) * factor, 0.0))


def add_branch(held_ref, weights_ref, scale, u_ref, unew_ref, onto_ref=None):
    put = placer(onto_ref) if onto_ref is not None else None
    for row, block in branch_blocks(held_ref, weights_ref):
        after = u_ref[row] + scale * block
        unew_ref[row] = after
        if put:
            put(row, after)


def split_weights(raw_ref, at, weights_ref):
    for across in range(3):
        first, middle, last = (raw_ref[at, up, across] for up in range(3))
        outer, inner = 0.5 * (first + last), 0.5 * middle
        for kind, value in enumerate((first, outer + inner, outer - inner, last)):
            high, low = split(value)
            weights_ref[kind, :, across * CHANNELS : (across + 1) * CHANNELS] = high
            weights_ref[kind, :, (3 + across) * CHANNELS : (4 + across) * CHANNELS] = low


def ready_kernel(initial_hbm, win_hbm, initial_ref, weights_ref, raw_ref, sem):
    weights = pltpu.make_async_copy(win_hbm.at[pl.ds(0, 1)], raw_ref, sem.at[0])
    state = pltpu.make_async_copy(initial_hbm, initial_ref, sem.at[1])
    weights.start()
    state.start()
    weights.wait()
    split_weights(raw_ref, 0, weights_ref)
    state.wait()


def open_kernel(initial_ref, before_ref, weights_ref, z_ref, u_ref, send_ref, held_ref):
    first = core() == 0
    put = placer(held_ref)
    for row in range(ROWS):
        value = jnp.where(first, initial_ref[row], before_ref[row])
        u_ref[row] = value
        put(row, value)
    into_conv(held_ref, weights_ref, z_ref, send_ref)


def fine_step(received_ref, z_ref, u_ref, ending_ref, begun_ref, unew_ref, znew_ref, send_ref, held_ref, onto_ref):
    normalise(received_ref, own_rows(received_ref), z_ref, held_ref)
    add_branch(held_ref, ending_ref, STEP_SIZE, u_ref, unew_ref, onto_ref)
    into_conv(onto_ref, begun_ref, znew_ref, send_ref)


def begin_kernel(
    received_ref, z_ref, u_ref, wout_ref, win_ref,
    unew_ref, znew_ref, send_ref, ending_ref, begun_ref, rest_ref, packed_ref, held_ref, onto_ref,
):
    split_weights(wout_ref, 0, ending_ref)
    normalise(received_ref, own_rows(received_ref), z_ref, held_ref)
    put = placer(onto_ref)
    for row, block in branch_blocks(held_ref, ending_ref):
        before = u_ref[row]
        after = before + STEP_SIZE * block
        unew_ref[row] = after
        put(row, after)
        coarse = before + FACTOR * STEP_SIZE * block
        rest_ref[row] = coarse - (before + FACTOR * (after - before))
    packed_ref[0] = win_ref[0]
    packed_ref[1] = wout_ref[0]
    split_weights(win_ref, 1, begun_ref)
    into_conv(onto_ref, begun_ref, znew_ref, send_ref)


def step_kernel(
    layer, received_ref, z_ref, u_ref, wout_ref, win_ref,
    unew_ref, znew_ref, send_ref, ending_ref, begun_ref, held_ref, onto_ref,
):
    split_weights(wout_ref, layer, ending_ref)
    normalise(received_ref, own_rows(received_ref), z_ref, held_ref)
    add_branch(held_ref, ending_ref, STEP_SIZE, u_ref, unew_ref, onto_ref)
    split_weights(win_ref, layer + 1, begun_ref)
    into_conv(onto_ref, begun_ref, znew_ref, send_ref)


def turn_kernel(
    received_ref, z_ref, u_ref, wout_ref, moved_ref,
    both_ref, ends_ref, send_ref, ending_ref, begun_ref, held_ref, onto_ref,
):
    split_weights(wout_ref, FACTOR - 1, ending_ref)
    normalise(received_ref, own_rows(received_ref), z_ref, held_ref)
    put = placer(onto_ref)
    for row, block in branch_blocks(held_ref, ending_ref):
        after = u_ref[row] + STEP_SIZE * block
        both_ref[0, row] = after
        ends_ref[row] = after
        put(row, after)
    split_weights(moved_ref, 0, begun_ref)
    into_conv(onto_ref, begun_ref, both_ref.at[1], send_ref)


def fork_kernel(
    received_ref, arrived_ref, both_ref, rest_ref, moved_ref, ending_ref, begun_ref,
    unew_ref, znew_ref, send_ref, held_ref, onto_ref,
):
    @pl.when(core() == 0)
    def _():
        put = placer(held_ref)
        for row in range(ROWS):
            value = both_ref[0, row] + rest_ref[row]
            unew_ref[row] = value
            put(row, value)
        into_conv(held_ref, moved_ref, znew_ref, send_ref)

    @pl.when(core() == 1)
    def _():
        normalise(received_ref, 0, arrived_ref.at[1], held_ref)
        add_branch(held_ref, ending_ref, STEP_SIZE, arrived_ref.at[0], unew_ref, onto_ref)
        into_conv(onto_ref, begun_ref, znew_ref, send_ref)


def coarse_kernel(
    received_ref, z_ref, u_ref, moved_ref, ending_ref, begun_ref,
    unew_ref, znew_ref, send_ref, held_ref, onto_ref, weights_ref,
):
    @pl.when(core() == 0)
    def _():
        split_weights(moved_ref, 1, weights_ref)
        normalise(received_ref, own_rows(received_ref), z_ref, held_ref)
        add_branch(held_ref, weights_ref, FACTOR * STEP_SIZE, u_ref, unew_ref)

    @pl.when(core() == 1)
    def _():
        fine_step(
            received_ref, z_ref, u_ref, ending_ref, begun_ref,
            unew_ref, znew_ref, send_ref, held_ref, onto_ref,
        )


def second_kernel(*refs):
    @pl.when(core() == 1)
    def _():
        fine_step(*refs)


def close_kernel(
    received_ref, z_ref, u_ref, ending_ref, arrived_ref, first_ref, coarse_ref, out_hbm,
    held_ref, out_ref, sem,
):
    @pl.when(core() == 0)
    def _():
        copy = pltpu.make_async_copy(first_ref, out_hbm, sem.at[0])
        copy.start()
        copy.wait()

    @pl.when(core() == 1)
    def _():
        normalise(received_ref, own_rows(received_ref), z_ref, held_ref)
        copies = []
        for row, block in branch_blocks(held_ref, ending_ref):
            fine = u_ref[row] + STEP_SIZE * block
            begun, first = arrived_ref[0, row], first_ref[row]
            tau = fine - (begun + FACTOR * (first - begun))
            out_ref[row] = coarse_ref[row] + tau
            if (row + 1) % (2 * PART) == 0:
                rows = pl.ds(row + 1 - 2 * PART, 2 * PART)
                copies.append(
                    pltpu.make_async_copy(out_ref.at[rows], out_hbm.at[rows], sem.at[len(copies)])
                )
                copies[-1].start()
        for copy in copies:
            copy.wait()


STATE = jax.ShapeDtypeStruct((ROWS, COLS, CHANNELS), jnp.float32)
BOTH = jax.ShapeDtypeStruct((2, ROWS, COLS, CHANNELS), jnp.float32)
VMEM = pl.BlockSpec(memory_space=pltpu.VMEM)
HELD = [pltpu.VMEM((4, PAIRS * COLS, 2 * CHANNELS), jnp.bfloat16)]
WEIGHTS = [pltpu.VMEM((4, CHANNELS, 6 * CHANNELS), jnp.bfloat16)]
READY = jax.ShapeDtypeStruct(WEIGHTS[0].shape, jnp.bfloat16)
TWO = HELD * 2
CLOSE = HELD + [
    pltpu.VMEM((ROWS, COLS, CHANNELS), jnp.float32),
    pltpu.SemaphoreType.DMA((CHUNKS,)),
]
CONV_FLOPS = 2 * 4 * 512 * 256 * 768


def call(kernel, name, outs, convs, scratch, *args, out_space=VMEM):
    touched = sum(a.size * a.dtype.itemsize for a in (*args, *outs))
    return pl.pallas_call(
        kernel,
        name=name,
        out_shape=tuple(outs),
        in_specs=[VMEM] * len(args),
        out_specs=(out_space,) * len(outs),
        scratch_shapes=scratch,
        compiler_params=pltpu.CompilerParams(vmem_limit_bytes=VMEM_LIMIT),
        cost_estimate=pl.CostEstimate(
            flops=convs * CONV_FLOPS, bytes_accessed=touched, transcendentals=0
        ),
    )(*args)


def ready(initial, conv_in):
    shape = conv_in.shape[1:]
    return pl.pallas_call(
        ready_kernel,
        name="ready",
        out_shape=(STATE, READY),
        in_specs=[pl.BlockSpec(memory_space=pltpu.HBM)] * 2,
        out_specs=(VMEM,) * 2,
        scratch_shapes=[
            pltpu.VMEM((1,) + shape, jnp.float32),
            pltpu.SemaphoreType.DMA((2,)),
        ],
        compiler_params=pltpu.CompilerParams(vmem_limit_bytes=READY_LIMIT),
        cost_estimate=pl.CostEstimate(flops=1000, bytes_accessed=3000000, transcendentals=0),
    )(*(pltpu.with_memory_space_constraint(x, pltpu.HBM) for x in (initial, conv_in)))


def swapped(x):
    return lax.ppermute(x, "depth", [(0, 1), (1, 0)])


def exchange(send):
    apart = send.reshape(send.shape[0] // 2, 2, CHANNELS)
    return lax.all_to_all(apart, WORLD, 0, 0).reshape(send.shape)


def body(initial, guess, conv_in, conv_out):
    devices = lax.axis_size(WORLD)
    sent = jax.ShapeDtypeStruct((2 * devices, CHANNELS), jnp.float32)
    outs = (STATE, STATE, sent)

    before = swapped(guess[0, 0])
    held, weights = ready(initial[0], conv_in)
    z, u, send = call(open_kernel, "open", outs, 1, HELD, held, before, weights)
    received = exchange(send)
    packed = jax.ShapeDtypeStruct((2,) + conv_in.shape[1:], jnp.float32)
    u, z, send, ending, begun, rest, packed = call(
        begin_kernel, "begin", outs + (READY, READY, STATE, packed), 2, TWO,
        received, z, u, conv_out, conv_in,
    )
    endings, beginnings = [ending], [None, begun]
    moved = swapped(packed)
    received = exchange(send)
    for layer in (1, 2):
        u, z, send, ending, begun = call(
            functools.partial(step_kernel, layer), "step", outs + (READY, READY), 2, TWO,
            received, z, u, conv_out, conv_in,
        )
        endings.append(ending)
        beginnings.append(begun)
        received = exchange(send)
    both, ends, send, ending, coarse_in = call(
        turn_kernel, "turn", (BOTH, STATE, sent, READY, READY), 2, TWO,
        received, z, u, conv_out, moved,
    )
    endings.append(ending)
    arrived = swapped(both)
    received = exchange(send)
    first, z, send = call(
        fork_kernel, "fork", outs, 2, TWO,
        received, arrived, both, rest, coarse_in, endings[0], beginnings[1],
    )
    received = exchange(send)
    u, z, send = call(
        coarse_kernel, "coarse", outs, 2, TWO + WEIGHTS,
        received, z, first, moved, endings[1], beginnings[2],
    )
    coarse = swapped(u)
    received = exchange(send)
    u, z, send = call(
        second_kernel, "second", outs, 2, TWO, received, z, u, endings[2], beginnings[3]
    )
    received = exchange(send)
    (result,) = call(
        close_kernel, "close", (STATE,), 1, CLOSE,
        received, z, u, endings[3], arrived, first, coarse,
        out_space=pl.BlockSpec(memory_space=pltpu.HBM),
    )
    return (result[None, None], ends[None, None])


def solution(mesh):
    split_mesh = Mesh(
        mesh.devices.reshape(mesh.shape["depth"], 4, 4, 4),
        ("depth", "batch_0", "batch_1", "batch_2"),
    )
    placed = (
        P(BATCH, None, None, None),
        P("depth", BATCH, None, None, None),
        P("depth", None, None, None, None),
        P("depth", None, None, None, None),
    )
    return jax.shard_map(
        body,
        mesh=split_mesh,
        in_specs=placed,
        out_specs=(P("depth", BATCH, None, None, None), P("depth", BATCH, None, None, None)),
        check_vma=False,
    )
```

```python
import functools

import jax
import jax.numpy as jnp
from jax import lax
from jax.experimental import pallas as pl
from jax.experimental.pallas import tpu as pltpu
from jax.sharding import Mesh
from jax.sharding import PartitionSpec as P

FACTOR = 4
BATCH = ("batch_0", "batch_1", "batch_2")
WORLD = ("depth",) + BATCH

EPSILON = 1e-05
STEP_SIZE = 0.25

ROWS = 32
COLS = 32
CHANNELS = 128
PAIRS = ROWS // 2
CELLS = ROWS * COLS
ENDING_PARTS = (10, 6)
BEGUN_PARTS = (9, 7)
VMEM_LIMIT = 24 * 2**20


def split(x):
    high = x.astype(jnp.bfloat16)
    low = (x - high.astype(jnp.float32)).astype(jnp.bfloat16)
    return high, low


def placer(held_ref):
    rows = {-1: jnp.zeros((COLS, CHANNELS), jnp.float32)}

    def put(pair):
        d0, d1, d2, d3 = (rows[2 * pair + i] for i in range(-1, 3))
        del rows[2 * pair - 1], rows[2 * pair]
        at = slice(pair * COLS, (pair + 1) * COLS)
        for kind, value in enumerate((d0 - d2, d1 + d2, d2 - d1, d1 - d3)):
            high, low = split(value)
            held_ref[kind, at, :CHANNELS] = high
            held_ref[kind, at, CHANNELS:] = low

    def add(row, value):
        rows[row] = value
        if row and row % 2 == 0:
            put(row // 2 - 1)
        if row == ROWS - 1:
            rows[ROWS] = rows_end
            put(PAIRS - 1)

    rows_end = rows[-1]
    return add


def convolve(held_ref, weights_ref, first, pairs):
    many = pairs * COLS
    at = slice(first * COLS, first * COLS + many)
    wide = 3 * CHANNELS

    def product(kind):
        right = weights_ref[kind]
        out = jnp.dot(
            held_ref[kind, at, :],
            jnp.concatenate([right, right], axis=0),
            preferred_element_type=jnp.float32,
        )
        return out[:, :wide] + out[:, wide:]

    m0, m1, m2, m3 = (product(kind) for kind in range(4))
    column = lax.broadcasted_iota(jnp.int32, (many, CHANNELS), 0) % COLS

    def across(x):
        left, middle, right = (x[:, i * CHANNELS : (i + 1) * CHANNELS] for i in range(3))
        out = middle + jnp.where(column == 0, 0.0, pltpu.roll(left, 1, 0))
        return out + jnp.where(column == COLS - 1, 0.0, pltpu.roll(right, many - 1, 0))

    return across(m0 + (m1 + m2)), across((m1 - m2) - m3)


def starts(parts):
    return [(sum(parts[:i]), pairs) for i, pairs in enumerate(parts)]


def branch_blocks(held_ref, weights_ref):
    for first, pairs in starts(ENDING_PARTS):
        halves = convolve(held_ref, weights_ref, first, pairs)
        for pair in range(pairs):
            for half in range(2):
                yield 2 * (first + pair) + half, halves[half][pair * COLS : (pair + 1) * COLS]


def into_conv(held_ref, weights_ref, z_ref, send_ref):
    totals, squares = [], []
    for first, pairs in starts(BEGUN_PARTS):
        cells = pairs * COLS
        for half, out in enumerate(convolve(held_ref, weights_ref, first, pairs)):
            for pair in range(pairs):
                z_ref[2 * (first + pair) + half] = out[pair * COLS : (pair + 1) * COLS]
            total = jnp.sum(out, axis=0, keepdims=True)
            away = out - total * (1.0 / cells)
            totals.append((total, cells))
            squares.append(jnp.sum(away * away, axis=0, keepdims=True))
    total = functools.reduce(jnp.add, [part for part, _ in totals])
    square = functools.reduce(jnp.add, squares)
    for part, cells in totals:
        away = part * (1.0 / cells) - total * (1.0 / CELLS)
        square = square + cells * (away * away)
    is_sum = lax.broadcasted_iota(jnp.int32, send_ref.shape, 0) % 2 == 0
    send_ref[...] = jnp.where(is_sum, total, square)


def core():
    return lax.axis_index("depth")


def own_rows(received_ref):
    return core() * (received_ref.shape[0] // 2)


def combined(received_ref, base):
    samples = received_ref.shape[0] // 4
    rows = received_ref[pl.ds(pl.multiple_of(base, 2 * samples), 2 * samples), :]
    is_sum = lax.broadcasted_iota(jnp.int32, rows.shape, 0) % 2 == 0
    average = jnp.sum(jnp.where(is_sum, rows, 0.0), axis=0, keepdims=True) * (1.0 / (samples * CELLS))
    away = rows * (1.0 / CELLS) - average
    square = jnp.sum(jnp.where(is_sum, CELLS * (away * away), rows), axis=0, keepdims=True)
    return average, lax.rsqrt(square * (1.0 / (samples * CELLS)) + EPSILON)


def normalise(received_ref, base, z_ref, held_ref):
    average, factor = combined(received_ref, base)
    put = placer(held_ref)
    for row in range(ROWS):
        put(row, jnp.maximum((z_ref[row] - average) * factor, 0.0))


def add_branch(held_ref, weights_ref, scale, u_ref, unew_ref, onto_ref=None):
    put = placer(onto_ref) if onto_ref is not None else None
    for row, block in branch_blocks(held_ref, weights_ref):
        after = u_ref[row] + scale * block
        unew_ref[row] = after
        if put:
            put(row, after)


def split_weights(raw_ref, at, weights_ref):
    for across in range(3):
        first, middle, last = (raw_ref[at, up, across] for up in range(3))
        outer, inner = 0.5 * (first + last), 0.5 * middle
        for kind, value in enumerate((first, outer + inner, outer - inner, last)):
            high, low = split(value)
            weights_ref[kind, :, across * CHANNELS : (across + 1) * CHANNELS] = high
            weights_ref[kind, :, (3 + across) * CHANNELS : (4 + across) * CHANNELS] = low


def ready_kernel(initial_hbm, win_hbm, wout_hbm, initial_ref, begun_ref, ending_ref, raw_ref, sem):
    weights = [
        pltpu.make_async_copy(hbm.at[0], raw_ref.at[at], sem.at[at])
        for at, hbm in enumerate((win_hbm, wout_hbm))
    ]
    state = pltpu.make_async_copy(initial_hbm, initial_ref, sem.at[2])
    for copy in (*weights, state):
        copy.start()
    for at, ready_ref in enumerate((begun_ref, ending_ref)):
        weights[at].wait()
        split_weights(raw_ref, at, ready_ref)
    state.wait()


def open_kernel(initial_ref, before_ref, weights_ref, z_ref, u_ref, send_ref, held_ref):
    first = core() == 0
    put = placer(held_ref)
    for row in range(ROWS):
        value = jnp.where(first, initial_ref[row], before_ref[row])
        u_ref[row] = value
        put(row, value)
    into_conv(held_ref, weights_ref, z_ref, send_ref)


def fine_step(received_ref, z_ref, u_ref, ending_ref, begun_ref, unew_ref, znew_ref, send_ref, held_ref, onto_ref):
    normalise(received_ref, own_rows(received_ref), z_ref, held_ref)
    add_branch(held_ref, ending_ref, STEP_SIZE, u_ref, unew_ref, onto_ref)
    into_conv(onto_ref, begun_ref, znew_ref, send_ref)


def begin_kernel(
    received_ref, z_ref, u_ref, ending_ref, wout_ref, win_ref,
    unew_ref, znew_ref, send_ref, begun_ref, rest_ref, packed_ref, held_ref, onto_ref,
):
    normalise(received_ref, own_rows(received_ref), z_ref, held_ref)
    put = placer(onto_ref)
    for row, block in branch_blocks(held_ref, ending_ref):
        before = u_ref[row]
        after = before + STEP_SIZE * block
        unew_ref[row] = after
        put(row, after)
        coarse = before + FACTOR * STEP_SIZE * block
        rest_ref[row] = coarse - (before + FACTOR * (after - before))
    packed_ref[0] = win_ref[0]
    packed_ref[1] = wout_ref[0]
    split_weights(win_ref, 1, begun_ref)
    into_conv(onto_ref, begun_ref, znew_ref, send_ref)


def step_kernel(
    layer, received_ref, z_ref, u_ref, wout_ref, win_ref,
    unew_ref, znew_ref, send_ref, ending_ref, begun_ref, held_ref, onto_ref,
):
    split_weights(wout_ref, layer, ending_ref)
    normalise(received_ref, own_rows(received_ref), z_ref, held_ref)
    add_branch(held_ref, ending_ref, STEP_SIZE, u_ref, unew_ref, onto_ref)
    split_weights(win_ref, layer + 1, begun_ref)
    into_conv(onto_ref, begun_ref, znew_ref, send_ref)


def turn_kernel(
    received_ref, z_ref, u_ref, wout_ref, moved_ref,
    both_ref, ends_ref, send_ref, ending_ref, begun_ref, held_ref, onto_ref,
):
    split_weights(wout_ref, FACTOR - 1, ending_ref)
    normalise(received_ref, own_rows(received_ref), z_ref, held_ref)
    put = placer(onto_ref)
    for row, block in branch_blocks(held_ref, ending_ref):
        after = u_ref[row] + STEP_SIZE * block
        both_ref[0, row] = after
        ends_ref[row] = after
        put(row, after)
    split_weights(moved_ref, 0, begun_ref)
    into_conv(onto_ref, begun_ref, both_ref.at[1], send_ref)


def fork_kernel(
    received_ref, arrived_ref, both_ref, rest_ref, moved_ref, ending_ref, begun_ref,
    unew_ref, znew_ref, send_ref, held_ref, onto_ref,
):
    @pl.when(core() == 0)
    def _():
        put = placer(held_ref)
        for row in range(ROWS):
            value = both_ref[0, row] + rest_ref[row]
            unew_ref[row] = value
            put(row, value)
        into_conv(held_ref, moved_ref, znew_ref, send_ref)

    @pl.when(core() == 1)
    def _():
        normalise(received_ref, 0, arrived_ref.at[1], held_ref)
        add_branch(held_ref, ending_ref, STEP_SIZE, arrived_ref.at[0], unew_ref, onto_ref)
        into_conv(onto_ref, begun_ref, znew_ref, send_ref)


def coarse_kernel(
    received_ref, z_ref, u_ref, moved_ref, ending_ref, begun_ref,
    unew_ref, znew_ref, send_ref, held_ref, onto_ref, weights_ref,
):
    @pl.when(core() == 0)
    def _():
        split_weights(moved_ref, 1, weights_ref)
        normalise(received_ref, own_rows(received_ref), z_ref, held_ref)
        add_branch(held_ref, weights_ref, FACTOR * STEP_SIZE, u_ref, unew_ref)

    @pl.when(core() == 1)
    def _():
        fine_step(
            received_ref, z_ref, u_ref, ending_ref, begun_ref,
            unew_ref, znew_ref, send_ref, held_ref, onto_ref,
        )


def second_kernel(*refs):
    @pl.when(core() == 1)
    def _():
        fine_step(*refs)


def close_kernel(
    received_ref, z_ref, u_ref, ending_ref, arrived_ref, first_ref, coarse_ref, out_hbm,
    held_ref, out_ref, sem,
):
    @pl.when(core() == 0)
    def _():
        copy = pltpu.make_async_copy(first_ref, out_hbm, sem.at[0])
        copy.start()
        copy.wait()

    @pl.when(core() == 1)
    def _():
        normalise(received_ref, own_rows(received_ref), z_ref, held_ref)
        copies = []
        for row, block in branch_blocks(held_ref, ending_ref):
            fine = u_ref[row] + STEP_SIZE * block
            begun, first = arrived_ref[0, row], first_ref[row]
            tau = fine - (begun + FACTOR * (first - begun))
            out_ref[row] = coarse_ref[row] + tau
            if (row + 1) % 8 == 0:
                rows = pl.ds(row - 7, 8)
                copies.append(
                    pltpu.make_async_copy(out_ref.at[rows], out_hbm.at[rows], sem.at[len(copies)])
                )
                copies[-1].start()
        for copy in copies:
            copy.wait()


STATE = jax.ShapeDtypeStruct((ROWS, COLS, CHANNELS), jnp.float32)
BOTH = jax.ShapeDtypeStruct((2, ROWS, COLS, CHANNELS), jnp.float32)
VMEM = pl.BlockSpec(memory_space=pltpu.VMEM)
HELD = [pltpu.VMEM((4, PAIRS * COLS, 2 * CHANNELS), jnp.bfloat16)]
WEIGHTS = [pltpu.VMEM((4, CHANNELS, 6 * CHANNELS), jnp.bfloat16)]
READY = jax.ShapeDtypeStruct(WEIGHTS[0].shape, jnp.bfloat16)
TWO = HELD * 2
CLOSE = HELD + [
    pltpu.VMEM((ROWS, COLS, CHANNELS), jnp.float32),
    pltpu.SemaphoreType.DMA((ROWS // 8,)),
]
CONV_FLOPS = 2 * 4 * 512 * 256 * 768


def call(kernel, name, outs, convs, scratch, *args, out_space=VMEM):
    touched = sum(a.size * a.dtype.itemsize for a in (*args, *outs))
    return pl.pallas_call(
        kernel,
        name=name,
        out_shape=tuple(outs),
        in_specs=[VMEM] * len(args),
        out_specs=(out_space,) * len(outs),
        scratch_shapes=scratch,
        compiler_params=pltpu.CompilerParams(vmem_limit_bytes=VMEM_LIMIT),
        cost_estimate=pl.CostEstimate(
            flops=convs * CONV_FLOPS, bytes_accessed=touched, transcendentals=0
        ),
    )(*args)


def ready(initial, conv_in, conv_out):
    shape = conv_in.shape[1:]
    return pl.pallas_call(
        ready_kernel,
        name="ready",
        out_shape=(STATE, READY, READY),
        in_specs=[pl.BlockSpec(memory_space=pltpu.HBM)] * 3,
        out_specs=(VMEM,) * 3,
        scratch_shapes=[
            pltpu.VMEM((2,) + shape, jnp.float32),
            pltpu.SemaphoreType.DMA((3,)),
        ],
        compiler_params=pltpu.CompilerParams(vmem_limit_bytes=VMEM_LIMIT),
        cost_estimate=pl.CostEstimate(flops=1000, bytes_accessed=4000000, transcendentals=0),
    )(*(pltpu.with_memory_space_constraint(x, pltpu.HBM) for x in (initial, conv_in, conv_out)))


def swapped(x):
    return lax.ppermute(x, "depth", [(0, 1), (1, 0)])


def exchange(send):
    apart = send.reshape(send.shape[0] // 2, 2, CHANNELS)
    return lax.all_to_all(apart, WORLD, 0, 0).reshape(send.shape)


def body(initial, guess, conv_in, conv_out):
    devices = lax.axis_size(WORLD)
    sent = jax.ShapeDtypeStruct((2 * devices, CHANNELS), jnp.float32)
    outs = (STATE, STATE, sent)

    before = swapped(guess[0, 0])
    held, weights, ending0 = ready(initial[0], conv_in, conv_out)
    before, conv_in, conv_out = lax.optimization_barrier((before, conv_in, conv_out))
    z, u, send = call(open_kernel, "open", outs, 1, HELD, held, before, weights)
    received = exchange(send)
    packed = jax.ShapeDtypeStruct((2,) + conv_in.shape[1:], jnp.float32)
    u, z, send, begun, rest, packed = call(
        begin_kernel, "begin", outs + (READY, STATE, packed), 2, TWO,
        received, z, u, ending0, conv_out, conv_in,
    )
    endings, beginnings = [ending0], [None, begun]
    moved = swapped(packed)
    received = exchange(send)
    for layer in (1, 2):
        u, z, send, ending, begun = call(
            functools.partial(step_kernel, layer), "step", outs + (READY, READY), 2, TWO,
            received, z, u, conv_out, conv_in,
        )
        endings.append(ending)
        beginnings.append(begun)
        received = exchange(send)
    both, ends, send, ending, coarse_in = call(
        turn_kernel, "turn", (BOTH, STATE, sent, READY, READY), 2, TWO,
        received, z, u, conv_out, moved,
    )
    endings.append(ending)
    arrived = swapped(both)
    received = exchange(send)
    first, z, send = call(
        fork_kernel, "fork", outs, 2, TWO,
        received, arrived, both, rest, coarse_in, endings[0], beginnings[1],
    )
    received = exchange(send)
    u, z, send = call(
        coarse_kernel, "coarse", outs, 2, TWO + WEIGHTS,
        received, z, first, moved, endings[1], beginnings[2],
    )
    coarse = swapped(u)
    received = exchange(send)
    u, z, send = call(
        second_kernel, "second", outs, 2, TWO, received, z, u, endings[2], beginnings[3]
    )
    received = exchange(send)
    (result,) = call(
        close_kernel, "close", (STATE,), 1, CLOSE,
        received, z, u, endings[3], arrived, first, coarse,
        out_space=pl.BlockSpec(memory_space=pltpu.HBM),
    )
    return (result[None, None], ends[None, None])


def solution(mesh):
    split_mesh = Mesh(
        mesh.devices.reshape(mesh.shape["depth"], 4, 4, 4),
        ("depth", "batch_0", "batch_1", "batch_2"),
    )
    placed = (
        P(BATCH, None, None, None),
        P("depth", BATCH, None, None, None),
        P("depth", None, None, None, None),
        P("depth", None, None, None, None),
    )
    return jax.shard_map(
        body,
        mesh=split_mesh,
        in_specs=placed,
        out_specs=(P("depth", BATCH, None, None, None), P("depth", BATCH, None, None, None)),
        check_vma=False,
    )
```

```python
import functools

import jax
import jax.numpy as jnp
from jax import lax
from jax.experimental import pallas as pl
from jax.experimental.pallas import tpu as pltpu
from jax.sharding import Mesh
from jax.sharding import PartitionSpec as P

FACTOR = 4
BATCH = ("batch_0", "batch_1", "batch_2")
WORLD = ("depth",) + BATCH

EPSILON = 1e-05
STEP_SIZE = 0.25

ROWS = 32
COLS = 32
CHANNELS = 128
PAIRS = ROWS // 2
CELLS = ROWS * COLS
CHUNKS = 2
PART = PAIRS // CHUNKS
VMEM_LIMIT = 24 * 2**20


def split(x):
    high = x.astype(jnp.bfloat16)
    low = (x - high.astype(jnp.float32)).astype(jnp.bfloat16)
    return high, low


def placer(held_ref):
    rows = {-1: jnp.zeros((COLS, CHANNELS), jnp.float32)}

    def put(pair):
        d0, d1, d2, d3 = (rows[2 * pair + i] for i in range(-1, 3))
        del rows[2 * pair - 1], rows[2 * pair]
        at = slice(pair * COLS, (pair + 1) * COLS)
        for kind, value in enumerate((d0 - d2, d1 + d2, d2 - d1, d1 - d3)):
            high, low = split(value)
            held_ref[kind, at, :CHANNELS] = high
            held_ref[kind, at, CHANNELS:] = low

    def add(row, value):
        rows[row] = value
        if row and row % 2 == 0:
            put(row // 2 - 1)
        if row == ROWS - 1:
            rows[ROWS] = rows_end
            put(PAIRS - 1)

    rows_end = rows[-1]
    return add


def convolve(held_ref, weights_ref, chunk):
    many = PART * COLS
    at = slice(chunk * many, (chunk + 1) * many)
    wide = 3 * CHANNELS

    def product(kind):
        right = weights_ref[kind]
        out = jnp.dot(
            held_ref[kind, at, :],
            jnp.concatenate([right, right], axis=0),
            preferred_element_type=jnp.float32,
        )
        return out[:, :wide] + out[:, wide:]

    m0, m1, m2, m3 = (product(kind) for kind in range(4))
    column = lax.broadcasted_iota(jnp.int32, (many, CHANNELS), 0) % COLS

    def across(x):
        left, middle, right = (x[:, i * CHANNELS : (i + 1) * CHANNELS] for i in range(3))
        out = middle + jnp.where(column == 0, 0.0, pltpu.roll(left, 1, 0))
        return out + jnp.where(column == COLS - 1, 0.0, pltpu.roll(right, many - 1, 0))

    return across(m0 + (m1 + m2)), across((m1 - m2) - m3)


def branch_blocks(held_ref, weights_ref):
    for chunk in range(CHUNKS):
        halves = convolve(held_ref, weights_ref, chunk)
        for pair in range(PART):
            for half in range(2):
                yield 2 * (chunk * PART + pair) + half, halves[half][pair * COLS : (pair + 1) * COLS]


def into_conv(held_ref, weights_ref, z_ref, send_ref):
    totals, squares = [], []
    for chunk in range(CHUNKS):
        halves = convolve(held_ref, weights_ref, chunk)
        for half, out in enumerate(halves):
            for pair in range(PART):
                z_ref[2 * (chunk * PART + pair) + half] = out[pair * COLS : (pair + 1) * COLS]
            total = jnp.sum(out, axis=0, keepdims=True)
            away = out - total * (1.0 / (PART * COLS))
            totals.append(total)
            squares.append(jnp.sum(away * away, axis=0, keepdims=True))
    total = functools.reduce(jnp.add, totals)
    square = functools.reduce(jnp.add, squares)
    for part in totals:
        away = part * (1.0 / (PART * COLS)) - total * (1.0 / CELLS)
        square = square + (PART * COLS) * (away * away)
    is_sum = lax.broadcasted_iota(jnp.int32, send_ref.shape, 0) % 2 == 0
    send_ref[...] = jnp.where(is_sum, total, square)


def core():
    return lax.axis_index("depth")


def own_rows(received_ref):
    return core() * (received_ref.shape[0] // 2)


def combined(received_ref, base):
    samples = received_ref.shape[0] // 4
    rows = received_ref[pl.ds(pl.multiple_of(base, 2 * samples), 2 * samples), :]
    is_sum = lax.broadcasted_iota(jnp.int32, rows.shape, 0) % 2 == 0
    average = jnp.sum(jnp.where(is_sum, rows, 0.0), axis=0, keepdims=True) * (1.0 / (samples * CELLS))
    away = rows * (1.0 / CELLS) - average
    square = jnp.sum(jnp.where(is_sum, CELLS * (away * away), rows), axis=0, keepdims=True)
    return average, lax.rsqrt(square * (1.0 / (samples * CELLS)) + EPSILON)


def normalise(received_ref, base, z_ref, held_ref):
    average, factor = combined(received_ref, base)
    put = placer(held_ref)
    for row in range(ROWS):
        put(row, jnp.maximum((z_ref[row] - average) * factor, 0.0))


def add_branch(held_ref, weights_ref, scale, u_ref, unew_ref, onto_ref=None):
    put = placer(onto_ref) if onto_ref is not None else None
    for row, block in branch_blocks(held_ref, weights_ref):
        after = u_ref[row] + scale * block
        unew_ref[row] = after
        if put:
            put(row, after)


def split_weights(raw_ref, at, weights_ref):
    for across in range(3):
        first, middle, last = (raw_ref[at, up, across] for up in range(3))
        outer, inner = 0.5 * (first + last), 0.5 * middle
        for kind, value in enumerate((first, outer + inner, outer - inner, last)):
            high, low = split(value)
            weights_ref[kind, :, across * CHANNELS : (across + 1) * CHANNELS] = high
            weights_ref[kind, :, (3 + across) * CHANNELS : (4 + across) * CHANNELS] = low


def ready_kernel(
    initial_hbm, win_hbm, wout_hbm, initial_ref, begun0_ref, ending0_ref, begun1_ref, raw_ref, sem
):
    weights = [
        pltpu.make_async_copy(source, raw_ref.at[at], sem.at[at])
        for at, source in enumerate((win_hbm.at[0], wout_hbm.at[0], win_hbm.at[1]))
    ]
    state = pltpu.make_async_copy(initial_hbm, initial_ref, sem.at[3])
    for copy in (*weights, state):
        copy.start()
    for at, ready_ref in enumerate((begun0_ref, ending0_ref, begun1_ref)):
        weights[at].wait()
        split_weights(raw_ref, at, ready_ref)
    state.wait()


def open_kernel(initial_ref, before_ref, weights_ref, z_ref, u_ref, send_ref, held_ref):
    first = core() == 0
    put = placer(held_ref)
    for row in range(ROWS):
        value = jnp.where(first, initial_ref[row], before_ref[row])
        u_ref[row] = value
        put(row, value)
    into_conv(held_ref, weights_ref, z_ref, send_ref)


def fine_step(received_ref, z_ref, u_ref, ending_ref, begun_ref, unew_ref, znew_ref, send_ref, held_ref, onto_ref):
    normalise(received_ref, own_rows(received_ref), z_ref, held_ref)
    add_branch(held_ref, ending_ref, STEP_SIZE, u_ref, unew_ref, onto_ref)
    into_conv(onto_ref, begun_ref, znew_ref, send_ref)


def begin_kernel(
    received_ref, z_ref, u_ref, ending_ref, begun_ref, wout_ref, win_ref,
    unew_ref, znew_ref, send_ref, rest_ref, packed_ref, held_ref, onto_ref,
):
    normalise(received_ref, own_rows(received_ref), z_ref, held_ref)
    put = placer(onto_ref)
    for row, block in branch_blocks(held_ref, ending_ref):
        before = u_ref[row]
        after = before + STEP_SIZE * block
        unew_ref[row] = after
        put(row, after)
        coarse = before + FACTOR * STEP_SIZE * block
        rest_ref[row] = coarse - (before + FACTOR * (after - before))
    packed_ref[0] = win_ref[0]
    packed_ref[1] = wout_ref[0]
    into_conv(onto_ref, begun_ref, znew_ref, send_ref)


def step_kernel(
    layer, received_ref, z_ref, u_ref, wout_ref, win_ref,
    unew_ref, znew_ref, send_ref, ending_ref, begun_ref, held_ref, onto_ref,
):
    split_weights(wout_ref, layer, ending_ref)
    normalise(received_ref, own_rows(received_ref), z_ref, held_ref)
    add_branch(held_ref, ending_ref, STEP_SIZE, u_ref, unew_ref, onto_ref)
    split_weights(win_ref, layer + 1, begun_ref)
    into_conv(onto_ref, begun_ref, znew_ref, send_ref)


def turn_kernel(
    received_ref, z_ref, u_ref, wout_ref, moved_ref,
    both_ref, ends_ref, send_ref, ending_ref, begun_ref, held_ref, onto_ref,
):
    split_weights(wout_ref, FACTOR - 1, ending_ref)
    normalise(received_ref, own_rows(received_ref), z_ref, held_ref)
    put = placer(onto_ref)
    for row, block in branch_blocks(held_ref, ending_ref):
        after = u_ref[row] + STEP_SIZE * block
        both_ref[0, row] = after
        ends_ref[row] = after
        put(row, after)
    split_weights(moved_ref, 0, begun_ref)
    into_conv(onto_ref, begun_ref, both_ref.at[1], send_ref)


def fork_kernel(
    received_ref, arrived_ref, both_ref, rest_ref, moved_ref, ending_ref, begun_ref,
    unew_ref, znew_ref, send_ref, held_ref, onto_ref,
):
    @pl.when(core() == 0)
    def _():
        put = placer(held_ref)
        for row in range(ROWS):
            value = both_ref[0, row] + rest_ref[row]
            unew_ref[row] = value
            put(row, value)
        into_conv(held_ref, moved_ref, znew_ref, send_ref)

    @pl.when(core() == 1)
    def _():
        normalise(received_ref, 0, arrived_ref.at[1], held_ref)
        add_branch(held_ref, ending_ref, STEP_SIZE, arrived_ref.at[0], unew_ref, onto_ref)
        into_conv(onto_ref, begun_ref, znew_ref, send_ref)


def coarse_kernel(
    received_ref, z_ref, u_ref, moved_ref, ending_ref, begun_ref,
    unew_ref, znew_ref, send_ref, held_ref, onto_ref, weights_ref,
):
    @pl.when(core() == 0)
    def _():
        split_weights(moved_ref, 1, weights_ref)
        normalise(received_ref, own_rows(received_ref), z_ref, held_ref)
        add_branch(held_ref, weights_ref, FACTOR * STEP_SIZE, u_ref, unew_ref)

    @pl.when(core() == 1)
    def _():
        fine_step(
            received_ref, z_ref, u_ref, ending_ref, begun_ref,
            unew_ref, znew_ref, send_ref, held_ref, onto_ref,
        )


def second_kernel(*refs):
    @pl.when(core() == 1)
    def _():
        fine_step(*refs)


def close_kernel(
    received_ref, z_ref, u_ref, ending_ref, arrived_ref, first_ref, coarse_ref, out_hbm,
    held_ref, out_ref, sem,
):
    @pl.when(core() == 0)
    def _():
        copy = pltpu.make_async_copy(first_ref, out_hbm, sem.at[0])
        copy.start()
        copy.wait()

    @pl.when(core() == 1)
    def _():
        normalise(received_ref, own_rows(received_ref), z_ref, held_ref)
        copies = []
        for row, block in branch_blocks(held_ref, ending_ref):
            fine = u_ref[row] + STEP_SIZE * block
            begun, first = arrived_ref[0, row], first_ref[row]
            tau = fine - (begun + FACTOR * (first - begun))
            out_ref[row] = coarse_ref[row] + tau
            if (row + 1) % (2 * PART) == 0:
                rows = pl.ds(row + 1 - 2 * PART, 2 * PART)
                copies.append(
                    pltpu.make_async_copy(out_ref.at[rows], out_hbm.at[rows], sem.at[len(copies)])
                )
                copies[-1].start()
        for copy in copies:
            copy.wait()


STATE = jax.ShapeDtypeStruct((ROWS, COLS, CHANNELS), jnp.float32)
BOTH = jax.ShapeDtypeStruct((2, ROWS, COLS, CHANNELS), jnp.float32)
VMEM = pl.BlockSpec(memory_space=pltpu.VMEM)
HELD = [pltpu.VMEM((4, PAIRS * COLS, 2 * CHANNELS), jnp.bfloat16)]
WEIGHTS = [pltpu.VMEM((4, CHANNELS, 6 * CHANNELS), jnp.bfloat16)]
READY = jax.ShapeDtypeStruct(WEIGHTS[0].shape, jnp.bfloat16)
TWO = HELD * 2
CLOSE = HELD + [
    pltpu.VMEM((ROWS, COLS, CHANNELS), jnp.float32),
    pltpu.SemaphoreType.DMA((CHUNKS,)),
]
CONV_FLOPS = 2 * 4 * 512 * 256 * 768


def call(kernel, name, outs, convs, scratch, *args, out_space=VMEM):
    touched = sum(a.size * a.dtype.itemsize for a in (*args, *outs))
    return pl.pallas_call(
        kernel,
        name=name,
        out_shape=tuple(outs),
        in_specs=[VMEM] * len(args),
        out_specs=(out_space,) * len(outs),
        scratch_shapes=scratch,
        compiler_params=pltpu.CompilerParams(vmem_limit_bytes=VMEM_LIMIT),
        cost_estimate=pl.CostEstimate(
            flops=convs * CONV_FLOPS, bytes_accessed=touched, transcendentals=0
        ),
    )(*args)


def ready(initial, conv_in, conv_out):
    shape = conv_in.shape[1:]
    return pl.pallas_call(
        ready_kernel,
        name="ready",
        out_shape=(STATE, READY, READY, READY),
        in_specs=[pl.BlockSpec(memory_space=pltpu.HBM)] * 3,
        out_specs=(VMEM,) * 4,
        scratch_shapes=[
            pltpu.VMEM((3,) + shape, jnp.float32),
            pltpu.SemaphoreType.DMA((4,)),
        ],
        compiler_params=pltpu.CompilerParams(vmem_limit_bytes=VMEM_LIMIT),
        cost_estimate=pl.CostEstimate(flops=1000, bytes_accessed=5000000, transcendentals=0),
    )(*(pltpu.with_memory_space_constraint(x, pltpu.HBM) for x in (initial, conv_in, conv_out)))


def swapped(x):
    return lax.ppermute(x, "depth", [(0, 1), (1, 0)])


def exchange(send):
    apart = send.reshape(send.shape[0] // 2, 2, CHANNELS)
    return lax.all_to_all(apart, WORLD, 0, 0).reshape(send.shape)


def body(initial, guess, conv_in, conv_out):
    devices = lax.axis_size(WORLD)
    sent = jax.ShapeDtypeStruct((2 * devices, CHANNELS), jnp.float32)
    outs = (STATE, STATE, sent)

    before = swapped(guess[0, 0])
    held, weights, ending0, begun1 = ready(initial[0], conv_in, conv_out)
    z, u, send = call(open_kernel, "open", outs, 1, HELD, held, before, weights)
    received = exchange(send)
    packed = jax.ShapeDtypeStruct((2,) + conv_in.shape[1:], jnp.float32)
    u, z, send, rest, packed = call(
        begin_kernel, "begin", outs + (STATE, packed), 2, TWO,
        received, z, u, ending0, begun1, conv_out, conv_in,
    )
    endings, beginnings = [ending0], [None, begun1]
    moved = swapped(packed)
    received = exchange(send)
    for layer in (1, 2):
        u, z, send, ending, begun = call(
            functools.partial(step_kernel, layer), "step", outs + (READY, READY), 2, TWO,
            received, z, u, conv_out, conv_in,
        )
        endings.append(ending)
        beginnings.append(begun)
        received = exchange(send)
    both, ends, send, ending, coarse_in = call(
        turn_kernel, "turn", (BOTH, STATE, sent, READY, READY), 2, TWO,
        received, z, u, conv_out, moved,
    )
    endings.append(ending)
    arrived = swapped(both)
    received = exchange(send)
    first, z, send = call(
        fork_kernel, "fork", outs, 2, TWO,
        received, arrived, both, rest, coarse_in, endings[0], beginnings[1],
    )
    received = exchange(send)
    u, z, send = call(
        coarse_kernel, "coarse", outs, 2, TWO + WEIGHTS,
        received, z, first, moved, endings[1], beginnings[2],
    )
    coarse = swapped(u)
    received = exchange(send)
    u, z, send = call(
        second_kernel, "second", outs, 2, TWO, received, z, u, endings[2], beginnings[3]
    )
    received = exchange(send)
    (result,) = call(
        close_kernel, "close", (STATE,), 1, CLOSE,
        received, z, u, endings[3], arrived, first, coarse,
        out_space=pl.BlockSpec(memory_space=pltpu.HBM),
    )
    return (result[None, None], ends[None, None])


def solution(mesh):
    split_mesh = Mesh(
        mesh.devices.reshape(mesh.shape["depth"], 4, 4, 4),
        ("depth", "batch_0", "batch_1", "batch_2"),
    )
    placed = (
        P(BATCH, None, None, None),
        P("depth", BATCH, None, None, None),
        P("depth", None, None, None, None),
        P("depth", None, None, None, None),
    )
    return jax.shard_map(
        body,
        mesh=split_mesh,
        in_specs=placed,
        out_specs=(P("depth", BATCH, None, None, None), P("depth", BATCH, None, None, None)),
        check_vma=False,
    )
```

```python
import functools

import jax
import jax.numpy as jnp
from jax import lax
from jax.experimental import pallas as pl
from jax.experimental.pallas import tpu as pltpu
from jax.sharding import Mesh
from jax.sharding import PartitionSpec as P

FACTOR = 4
BATCH = ("batch_0", "batch_1", "batch_2")
WORLD = ("depth",) + BATCH

EPSILON = 1e-05
STEP_SIZE = 0.25

ROWS = 32
COLS = 32
CHANNELS = 128
PAIRS = ROWS // 2
CELLS = ROWS * COLS
CHUNKS = 2
PART = PAIRS // CHUNKS
VMEM_LIMIT = 24 * 2**20


def split(x):
    high = x.astype(jnp.bfloat16)
    low = (x - high.astype(jnp.float32)).astype(jnp.bfloat16)
    return high, low


def placer(held_ref):
    rows = {-1: jnp.zeros((COLS, CHANNELS), jnp.float32)}

    def put(pair):
        d0, d1, d2, d3 = (rows[2 * pair + i] for i in range(-1, 3))
        del rows[2 * pair - 1], rows[2 * pair]
        at = slice(pair * COLS, (pair + 1) * COLS)
        for kind, value in enumerate((d0 - d2, d1 + d2, d2 - d1, d1 - d3)):
            high, low = split(value)
            held_ref[kind, at, :CHANNELS] = high
            held_ref[kind, at, CHANNELS:] = low

    def add(row, value):
        rows[row] = value
        if row and row % 2 == 0:
            put(row // 2 - 1)
        if row == ROWS - 1:
            rows[ROWS] = rows_end
            put(PAIRS - 1)

    rows_end = rows[-1]
    return add


def convolve(held_ref, weights_ref, chunk):
    many = PART * COLS
    at = slice(chunk * many, (chunk + 1) * many)
    wide = 3 * CHANNELS

    def product(kind):
        right = weights_ref[kind]
        out = jnp.dot(
            held_ref[kind, at, :],
            jnp.concatenate([right, right], axis=0),
            preferred_element_type=jnp.float32,
        )
        return out[:, :wide] + out[:, wide:]

    m0, m1, m2, m3 = (product(kind) for kind in range(4))
    column = lax.broadcasted_iota(jnp.int32, (many, CHANNELS), 0) % COLS

    def across(x):
        left, middle, right = (x[:, i * CHANNELS : (i + 1) * CHANNELS] for i in range(3))
        out = middle + jnp.where(column == 0, 0.0, pltpu.roll(left, 1, 0))
        return out + jnp.where(column == COLS - 1, 0.0, pltpu.roll(right, many - 1, 0))

    return across(m0 + (m1 + m2)), across((m1 - m2) - m3)


def branch_blocks(held_ref, weights_ref):
    for chunk in range(CHUNKS):
        halves = convolve(held_ref, weights_ref, chunk)
        for pair in range(PART):
            for half in range(2):
                yield 2 * (chunk * PART + pair) + half, halves[half][pair * COLS : (pair + 1) * COLS]


def into_conv(held_ref, weights_ref, z_ref, send_ref):
    totals, squares = [], []
    for chunk in range(CHUNKS):
        halves = convolve(held_ref, weights_ref, chunk)
        for half, out in enumerate(halves):
            for pair in range(PART):
                z_ref[2 * (chunk * PART + pair) + half] = out[pair * COLS : (pair + 1) * COLS]
            total = jnp.sum(out, axis=0, keepdims=True)
            away = out - total * (1.0 / (PART * COLS))
            totals.append(total)
            squares.append(jnp.sum(away * away, axis=0, keepdims=True))
    total = functools.reduce(jnp.add, totals)
    square = functools.reduce(jnp.add, squares)
    for part in totals:
        away = part * (1.0 / (PART * COLS)) - total * (1.0 / CELLS)
        square = square + (PART * COLS) * (away * away)
    is_sum = lax.broadcasted_iota(jnp.int32, send_ref.shape, 0) % 2 == 0
    send_ref[...] = jnp.where(is_sum, total, square)


def core():
    return lax.axis_index("depth")


def own_rows(received_ref):
    return core() * (received_ref.shape[0] // 2)


def combined(received_ref, base):
    samples = received_ref.shape[0] // 4
    rows = received_ref[pl.ds(pl.multiple_of(base, 2 * samples), 2 * samples), :]
    is_sum = lax.broadcasted_iota(jnp.int32, rows.shape, 0) % 2 == 0
    average = jnp.sum(jnp.where(is_sum, rows, 0.0), axis=0, keepdims=True) * (1.0 / (samples * CELLS))
    away = rows * (1.0 / CELLS) - average
    square = jnp.sum(jnp.where(is_sum, CELLS * (away * away), rows), axis=0, keepdims=True)
    return average, lax.rsqrt(square * (1.0 / (samples * CELLS)) + EPSILON)


def normalise(received_ref, base, z_ref, held_ref):
    average, factor = combined(received_ref, base)
    put = placer(held_ref)
    for row in range(ROWS):
        put(row, jnp.maximum((z_ref[row] - average) * factor, 0.0))


def add_branch(held_ref, weights_ref, scale, u_ref, unew_ref, onto_ref=None):
    put = placer(onto_ref) if onto_ref is not None else None
    for row, block in branch_blocks(held_ref, weights_ref):
        after = u_ref[row] + scale * block
        unew_ref[row] = after
        if put:
            put(row, after)


def split_weights(raw_ref, at, weights_ref):
    for across in range(3):
        first, middle, last = (raw_ref[at, up, across] for up in range(3))
        outer, inner = 0.5 * (first + last), 0.5 * middle
        for kind, value in enumerate((first, outer + inner, outer - inner, last)):
            high, low = split(value)
            weights_ref[kind, :, across * CHANNELS : (across + 1) * CHANNELS] = high
            weights_ref[kind, :, (3 + across) * CHANNELS : (4 + across) * CHANNELS] = low


def ready_kernel(
    initial_hbm, win_hbm, wout_hbm, initial_ref, begun0_ref, ending0_ref, begun1_ref, raw_ref, sem
):
    weights = [
        pltpu.make_async_copy(source, raw_ref.at[at], sem.at[at])
        for at, source in enumerate((win_hbm.at[0], wout_hbm.at[0], win_hbm.at[1]))
    ]
    state = pltpu.make_async_copy(initial_hbm, initial_ref, sem.at[3])
    for copy in (*weights, state):
        copy.start()
    for at, ready_ref in enumerate((begun0_ref, ending0_ref, begun1_ref)):
        weights[at].wait()
        split_weights(raw_ref, at, ready_ref)
    state.wait()


def open_kernel(initial_ref, before_ref, weights_ref, z_ref, u_ref, send_ref, held_ref):
    first = core() == 0
    put = placer(held_ref)
    for row in range(ROWS):
        value = jnp.where(first, initial_ref[row], before_ref[row])
        u_ref[row] = value
        put(row, value)
    into_conv(held_ref, weights_ref, z_ref, send_ref)


def fine_step(received_ref, z_ref, u_ref, ending_ref, begun_ref, unew_ref, znew_ref, send_ref, held_ref, onto_ref):
    normalise(received_ref, own_rows(received_ref), z_ref, held_ref)
    add_branch(held_ref, ending_ref, STEP_SIZE, u_ref, unew_ref, onto_ref)
    into_conv(onto_ref, begun_ref, znew_ref, send_ref)


def begin_kernel(
    received_ref, z_ref, u_ref, ending_ref, begun_ref, wout_ref, win_ref,
    unew_ref, znew_ref, send_ref, rest_ref, packed_ref, held_ref, onto_ref,
):
    normalise(received_ref, own_rows(received_ref), z_ref, held_ref)
    put = placer(onto_ref)
    for row, block in branch_blocks(held_ref, ending_ref):
        before = u_ref[row]
        after = before + STEP_SIZE * block
        unew_ref[row] = after
        put(row, after)
        coarse = before + FACTOR * STEP_SIZE * block
        rest_ref[row] = coarse - (before + FACTOR * (after - before))
    packed_ref[0] = win_ref[0]
    packed_ref[1] = wout_ref[0]
    into_conv(onto_ref, begun_ref, znew_ref, send_ref)


def step_kernel(
    layer, received_ref, z_ref, u_ref, wout_ref, win_ref,
    unew_ref, znew_ref, send_ref, ending_ref, begun_ref, held_ref, onto_ref,
):
    split_weights(wout_ref, layer, ending_ref)
    normalise(received_ref, own_rows(received_ref), z_ref, held_ref)
    add_branch(held_ref, ending_ref, STEP_SIZE, u_ref, unew_ref, onto_ref)
    split_weights(win_ref, layer + 1, begun_ref)
    into_conv(onto_ref, begun_ref, znew_ref, send_ref)


def turn_kernel(
    received_ref, z_ref, u_ref, wout_ref, moved_ref,
    both_ref, send_ref, ending_ref, begun_ref, held_ref, onto_ref,
):
    split_weights(wout_ref, FACTOR - 1, ending_ref)
    normalise(received_ref, own_rows(received_ref), z_ref, held_ref)
    put = placer(onto_ref)
    for row, block in branch_blocks(held_ref, ending_ref):
        after = u_ref[row] + STEP_SIZE * block
        both_ref[0, row] = after
        put(row, after)
    split_weights(moved_ref, 0, begun_ref)
    into_conv(onto_ref, begun_ref, both_ref.at[1], send_ref)


def fork_kernel(
    received_ref, arrived_ref, both_ref, rest_ref, moved_ref, ending_ref, begun_ref,
    unew_ref, znew_ref, send_ref, ends_hbm, held_ref, onto_ref, sem,
):
    ends = pltpu.make_async_copy(both_ref.at[0], ends_hbm, sem)
    ends.start()

    @pl.when(core() == 0)
    def _():
        put = placer(held_ref)
        for row in range(ROWS):
            value = both_ref[0, row] + rest_ref[row]
            unew_ref[row] = value
            put(row, value)
        into_conv(held_ref, moved_ref, znew_ref, send_ref)

    @pl.when(core() == 1)
    def _():
        normalise(received_ref, 0, arrived_ref.at[1], held_ref)
        add_branch(held_ref, ending_ref, STEP_SIZE, arrived_ref.at[0], unew_ref, onto_ref)
        into_conv(onto_ref, begun_ref, znew_ref, send_ref)

    ends.wait()


def coarse_kernel(
    received_ref, z_ref, u_ref, moved_ref, ending_ref, begun_ref,
    unew_ref, znew_ref, send_ref, held_ref, onto_ref, weights_ref,
):
    @pl.when(core() == 0)
    def _():
        split_weights(moved_ref, 1, weights_ref)
        normalise(received_ref, own_rows(received_ref), z_ref, held_ref)
        add_branch(held_ref, weights_ref, FACTOR * STEP_SIZE, u_ref, unew_ref)

    @pl.when(core() == 1)
    def _():
        fine_step(
            received_ref, z_ref, u_ref, ending_ref, begun_ref,
            unew_ref, znew_ref, send_ref, held_ref, onto_ref,
        )


def second_kernel(*refs):
    @pl.when(core() == 1)
    def _():
        fine_step(*refs)


def close_kernel(
    received_ref, z_ref, u_ref, ending_ref, arrived_ref, first_ref, coarse_ref, out_hbm,
    held_ref, out_ref, sem,
):
    @pl.when(core() == 0)
    def _():
        copy = pltpu.make_async_copy(first_ref, out_hbm, sem.at[0])
        copy.start()
        copy.wait()

    @pl.when(core() == 1)
    def _():
        normalise(received_ref, own_rows(received_ref), z_ref, held_ref)
        copies = []
        for row, block in branch_blocks(held_ref, ending_ref):
            fine = u_ref[row] + STEP_SIZE * block
            begun, first = arrived_ref[0, row], first_ref[row]
            tau = fine - (begun + FACTOR * (first - begun))
            out_ref[row] = coarse_ref[row] + tau
            if (row + 1) % (2 * PART) == 0:
                rows = pl.ds(row + 1 - 2 * PART, 2 * PART)
                copies.append(
                    pltpu.make_async_copy(out_ref.at[rows], out_hbm.at[rows], sem.at[len(copies)])
                )
                copies[-1].start()
        for copy in copies:
            copy.wait()


STATE = jax.ShapeDtypeStruct((ROWS, COLS, CHANNELS), jnp.float32)
BOTH = jax.ShapeDtypeStruct((2, ROWS, COLS, CHANNELS), jnp.float32)
VMEM = pl.BlockSpec(memory_space=pltpu.VMEM)
HBM = pl.BlockSpec(memory_space=pltpu.HBM)
HELD = [pltpu.VMEM((4, PAIRS * COLS, 2 * CHANNELS), jnp.bfloat16)]
WEIGHTS = [pltpu.VMEM((4, CHANNELS, 6 * CHANNELS), jnp.bfloat16)]
READY = jax.ShapeDtypeStruct(WEIGHTS[0].shape, jnp.bfloat16)
TWO = HELD * 2
CLOSE = HELD + [
    pltpu.VMEM((ROWS, COLS, CHANNELS), jnp.float32),
    pltpu.SemaphoreType.DMA((CHUNKS,)),
]
CONV_FLOPS = 2 * 4 * 512 * 256 * 768


def call(kernel, name, outs, convs, scratch, *args, spaces=None):
    touched = sum(a.size * a.dtype.itemsize for a in (*args, *outs))
    return pl.pallas_call(
        kernel,
        name=name,
        out_shape=tuple(outs),
        in_specs=[VMEM] * len(args),
        out_specs=spaces or (VMEM,) * len(outs),
        scratch_shapes=scratch,
        compiler_params=pltpu.CompilerParams(vmem_limit_bytes=VMEM_LIMIT),
        cost_estimate=pl.CostEstimate(
            flops=convs * CONV_FLOPS, bytes_accessed=touched, transcendentals=0
        ),
    )(*args)


def ready(initial, conv_in, conv_out):
    shape = conv_in.shape[1:]
    return pl.pallas_call(
        ready_kernel,
        name="ready",
        out_shape=(STATE, READY, READY, READY),
        in_specs=[pl.BlockSpec(memory_space=pltpu.HBM)] * 3,
        out_specs=(VMEM,) * 4,
        scratch_shapes=[
            pltpu.VMEM((3,) + shape, jnp.float32),
            pltpu.SemaphoreType.DMA((4,)),
        ],
        compiler_params=pltpu.CompilerParams(vmem_limit_bytes=VMEM_LIMIT),
        cost_estimate=pl.CostEstimate(flops=1000, bytes_accessed=5000000, transcendentals=0),
    )(*(pltpu.with_memory_space_constraint(x, pltpu.HBM) for x in (initial, conv_in, conv_out)))


def swapped(x):
    return lax.ppermute(x, "depth", [(0, 1), (1, 0)])


def exchange(send):
    apart = send.reshape(send.shape[0] // 2, 2, CHANNELS)
    return lax.all_to_all(apart, WORLD, 0, 0).reshape(send.shape)


def body(initial, guess, conv_in, conv_out):
    devices = lax.axis_size(WORLD)
    sent = jax.ShapeDtypeStruct((2 * devices, CHANNELS), jnp.float32)
    outs = (STATE, STATE, sent)

    before = swapped(guess[0, 0])
    held, weights, ending0, begun1 = ready(initial[0], conv_in, conv_out)
    z, u, send = call(open_kernel, "open", outs, 1, HELD, held, before, weights)
    received = exchange(send)
    packed = jax.ShapeDtypeStruct((2,) + conv_in.shape[1:], jnp.float32)
    u, z, send, rest, packed = call(
        begin_kernel, "begin", outs + (STATE, packed), 2, TWO,
        received, z, u, ending0, begun1, conv_out, conv_in,
    )
    endings, beginnings = [ending0], [None, begun1]
    moved = swapped(packed)
    received = exchange(send)
    for layer in (1, 2):
        u, z, send, ending, begun = call(
            functools.partial(step_kernel, layer), "step", outs + (READY, READY), 2, TWO,
            received, z, u, conv_out, conv_in,
        )
        endings.append(ending)
        beginnings.append(begun)
        received = exchange(send)
    both, send, ending, coarse_in = call(
        turn_kernel, "turn", (BOTH, sent, READY, READY), 2, TWO,
        received, z, u, conv_out, moved,
    )
    endings.append(ending)
    arrived = swapped(both)
    received = exchange(send)
    first, z, send, ends = call(
        fork_kernel, "fork", outs + (STATE,), 2, TWO + [pltpu.SemaphoreType.DMA(())],
        received, arrived, both, rest, coarse_in, endings[0], beginnings[1],
        spaces=(VMEM, VMEM, VMEM, HBM),
    )
    received = exchange(send)
    u, z, send = call(
        coarse_kernel, "coarse", outs, 2, TWO + WEIGHTS,
        received, z, first, moved, endings[1], beginnings[2],
    )
    coarse = swapped(u)
    received = exchange(send)
    u, z, send = call(
        second_kernel, "second", outs, 2, TWO, received, z, u, endings[2], beginnings[3]
    )
    received = exchange(send)
    (result,) = call(
        close_kernel, "close", (STATE,), 1, CLOSE,
        received, z, u, endings[3], arrived, first, coarse,
        spaces=(HBM,),
    )
    return (result[None, None], ends[None, None])


def solution(mesh):
    split_mesh = Mesh(
        mesh.devices.reshape(mesh.shape["depth"], 4, 4, 4),
        ("depth", "batch_0", "batch_1", "batch_2"),
    )
    placed = (
        P(BATCH, None, None, None),
        P("depth", BATCH, None, None, None),
        P("depth", None, None, None, None),
        P("depth", None, None, None, None),
    )
    return jax.shard_map(
        body,
        mesh=split_mesh,
        in_specs=placed,
        out_specs=(P("depth", BATCH, None, None, None), P("depth", BATCH, None, None, None)),
        check_vma=False,
    )
```
